256 devices in a mesh: tile: 32 (over y, z_hi, core), lev: 8 (over z_lo, x).
Axes of the slice: x: 4, y: 4, z: 8 (z_hi: 4, z_lo: 2; z = z_hi * 2 + z_lo), core: 2. Of those that a mesh axis runs over, the one named last changes fastest.
Arguments:
- state_in: float32 [128, 8192, 128], P('lev', 'tile'), may hold values from -6 to 6
- east_speed: bfloat16 [128, 8192, 128], P('lev', 'tile'), may hold values from -0.19921875 to 0.19921875
- north_speed: bfloat16 [128, 8192, 128], P('lev', 'tile'), may hold values from -0.19921875 to 0.19921875
- w_in: bfloat16 [128, 1024], replicated, may hold values from -0.5 to 0.5
- w_out: bfloat16 [128, 1024], replicated, may hold values from -0.1875 to 0.1875
- cotangent: float32 [128, 8192, 128], P('lev', 'tile'), may hold values from -6 to 6
Outputs:
- state_out: float32 [128, 8192, 128], P('lev', 'tile')
- state_grad: float32 [128, 8192, 128], P('lev', 'tile')
- w_in_grad: float32 [128, 1024], replicated
- w_out_grad: float32 [128, 1024], replicated
The draws below stay inside these ranges and needn't reach their ends.
All inputs are finite; a program needn't handle non-finite values.
Results may differ from the reference program's by a relative error of at most 0.0053.
Values may be sent and summed in bfloat16 or wider, within the bound.
No kernel may reach another device: no remote copies, remote signals or barrier semaphores. Data moves between devices by JAX's collectives and lax.ppermute only.
A program may use at most 128 MiB of HBM per device.

```python
import math
import jax
import jax.numpy as jnp
from jax import lax

LEV = 128
HID = 1024
CX = 256
CY = 128
NX = 8192
N_TILE = 32


def block_levels(rng, shape, split, smallest, high):
    def one(dim, shards_of):
        draws = jax.random.uniform(jax.random.fold_in(jax.random.fold_in(rng, 6), dim), (shards_of,), jnp.float32, smallest / len(split), high / len(split))
        return jnp.repeat(jnp.exp(draws), shape[dim] // shards_of).reshape((-1,) + (1,) * (len(shape) - dim - 1))

    factor_of = one(*split[0])
    for cut in split[1:]:
        factor_of = factor_of * one(*cut)
    return factor_of


def gaussian(own_key, shape, spread, reach, split=(), dtype=jnp.bfloat16):
    values = jax.random.normal(own_key, shape, jnp.float32) * spread
    if len(split) > 0:
        values = block_levels(own_key, shape, split, -0.22, 0.18) * values
    return jnp.clip(values, min=-reach, max=reach).astype(dtype)


def setup_inputs(seed: int = 0) -> dict:
    seeds = jax.random.split(jax.random.key(seed), 7)
    return {
        "state_in": gaussian(seeds[0], (LEV, NX, CY), 1.0, 6.0, ((0, 8), (1, 32)), jnp.float32),
        "east_speed": jnp.clip(jax.random.uniform(seeds[1], (LEV, NX, CY), jnp.float32, -0.19921875, 0.19921875) * block_levels(seeds[1], (LEV, NX, CY), ((0, 8), (1, 32)), -0.4, 0.0), -0.19921875, 0.19921875).astype(jnp.bfloat16),
        "north_speed": jnp.clip(jax.random.uniform(seeds[2], (LEV, NX, CY), jnp.float32, -0.19921875, 0.19921875) * block_levels(seeds[2], (LEV, NX, CY), ((0, 8), (1, 32)), -0.4, 0.0), -0.19921875, 0.19921875).astype(jnp.bfloat16),
        "w_in": gaussian(seeds[3], (LEV, HID), LEV ** -0.5, 0.5),
        "w_out": gaussian(seeds[4], (LEV, HID), HID ** -0.5, 0.1875),
        "cotangent": gaussian(seeds[5], (LEV, NX, CY), 1.0, 6.0, ((0, 8), (1, 32)), jnp.float32),
    }


KAPPA = 0.05
SLOPE_C = 0.7978845608028654
CUBIC = 0.044715

def gelu_slope(preact):
    tangent = jnp.tanh(SLOPE_C * (preact + CUBIC * preact * preact * preact))
    value = 0.5 * preact * (1.0 + tangent)
    slope = 0.5 * (1.0 + tangent) + 0.5 * preact * (1.0 - tangent * tangent) * SLOPE_C * (1.0 + 3.0 * CUBIC * preact * preact)
    return (value, slope)

def shift_up(values):
    return jnp.concatenate([values[:, :, 1:], jnp.zeros_like(values[:, :, :1])], 2)

def shift_down(values):
    return jnp.concatenate([jnp.zeros_like(values[:, :, :1]), values[:, :, :-1]], 2)

def north_parts(north_speed):
    north = north_speed.astype(jnp.float32)
    width = north.shape[2]
    wall = (jnp.arange(width) < width - 1).astype(jnp.float32)
    return (jnp.maximum(north, 0.0) * wall, jnp.minimum(north, 0.0) * wall)

def advance(quantity, east_speed, north_speed):
    east = east_speed.astype(jnp.float32)
    pos_east = jnp.maximum(east, 0.0)
    neg_east = jnp.minimum(east, 0.0)
    pos_north, neg_north = north_parts(north_speed)
    beyond = jnp.roll(quantity, -1, 1)
    behind = jnp.roll(quantity, 1, 1)
    east_flux = pos_east * quantity + neg_east * beyond
    west_flux = jnp.roll(pos_east, 1, 1) * behind + jnp.roll(neg_east, 1, 1) * quantity
    north_flux = pos_north * quantity + neg_north * shift_up(quantity)
    south_flux = shift_down(north_flux)
    return quantity - (east_flux - west_flux) - (north_flux - south_flux) + KAPPA * (beyond - 2.0 * quantity + behind)

def transpose_step(grad, east_speed, north_speed):
    east = east_speed.astype(jnp.float32)
    pos_east = jnp.maximum(east, 0.0)
    neg_west = jnp.roll(jnp.minimum(east, 0.0), 1, 1)
    pos_north, neg_north = north_parts(north_speed)
    beyond = jnp.roll(grad, -1, 1)
    behind = jnp.roll(grad, 1, 1)
    along = pos_east * (beyond - grad) + neg_west * (grad - behind)
    across = pos_north * (shift_up(grad) - grad) + shift_down(neg_north) * (grad - shift_down(grad))
    return grad + along + across + KAPPA * (beyond - 2.0 * grad + behind)

def to_blocks(values):
    return values.reshape(LEV, N_TILE, CX, CY).transpose(1, 0, 2, 3)

def from_blocks(values):
    return values.transpose(1, 0, 2, 3).reshape(LEV, NX, CY)

def widen(values):
    return lax.optimization_barrier(values.astype(jnp.bfloat16)).astype(jnp.float32)

def reference(state_in, east_speed, north_speed, w_in, w_out, cotangent):
    w_in_f = w_in.astype(jnp.float32)
    w_out_f = w_out.astype(jnp.float32)
    first = advance(state_in, east_speed, north_speed)
    columns = first.astype(jnp.bfloat16)

    def hidden_of(block):
        pre = jnp.einsum('lxy,lh->xyh', block.astype(jnp.float32), w_in_f)
        return gelu_slope(pre)

    def forward_block(block):
        act, slope = hidden_of(block)
        tend = jnp.einsum('xyh,lh->lxy', widen(act), w_out_f)
        return tend.astype(jnp.bfloat16)
    tendency = from_blocks(lax.map(forward_block, to_blocks(columns)))
    second = first + tendency.astype(jnp.float32)
    state_out = advance(second, east_speed, north_speed)
    back_two = transpose_step(cotangent, east_speed, north_speed)
    back_cols = back_two.astype(jnp.bfloat16)

    def backward_block(pair):
        block, gblock = pair
        act, slope = hidden_of(block)
        act_f = widen(act)
        gf = gblock.astype(jnp.float32)
        out_grad = jnp.einsum('lxy,xyh->lh', gf, act_f)
        d_act = jnp.einsum('lxy,lh->xyh', gf, w_out_f)
        d_pre = widen(d_act * slope)
        in_grad = jnp.einsum('lxy,xyh->lh', block.astype(jnp.float32), d_pre)
        d_cols = jnp.einsum('xyh,lh->lxy', d_pre, w_in_f).astype(jnp.bfloat16)
        return (d_cols, in_grad, out_grad)
    d_cols, in_parts, out_parts = lax.map(backward_block, (to_blocks(columns), to_blocks(back_cols)))
    back_one = back_two + from_blocks(d_cols).astype(jnp.float32)
    state_grad = transpose_step(back_one, east_speed, north_speed)
    scale = 1.0 / math.sqrt(NX * CY)
    w_in_grad = lax.optimization_barrier(jnp.sum(in_parts, 0)) * scale
    w_out_grad = lax.optimization_barrier(jnp.sum(out_parts, 0)) * scale
    return (state_out, state_grad, w_in_grad, w_out_grad)
```

```python
import functools
import math

import jax
import jax.numpy as jnp
from jax import lax
from jax.experimental import pallas as pl
from jax.experimental.pallas import tpu as pltpu
from jax.sharding import PartitionSpec as P

KAPPA = 0.05
SLOPE_C = 0.7978845608028654
CUBIC = 0.044715
ROWS = 32
F32 = jnp.float32
BF16 = jnp.bfloat16
VMEM_LIMIT = 48 * 1024 * 1024


def rows_at(ref, index, stride):
    return jnp.concatenate(
        [ref[pl.ds(index, 8, stride), :], ref[pl.ds(index + 8 * stride, 8, stride), :]], 0
    )


def put_rows(ref, index, stride, value):
    ref[pl.ds(index, 8, stride), :] = value[:8]
    ref[pl.ds(index + 8 * stride, 8, stride), :] = value[8:]


def up_of(value):
    return pltpu.roll(value, value.shape[1] - 1, 1)


def down_of(value):
    return pltpu.roll(value, 1, 1)


def wall_mask(north):
    lane = lax.broadcasted_iota(jnp.int32, north.shape, 1)
    return jnp.where(lane < north.shape[1] - 1, north, 0.0)


def step_row(q, q_next, g, g_next, east, north, flux, drift):
    north = wall_mask(north)
    pos_east = jnp.maximum(east, 0.0) + KAPPA
    neg_east = jnp.minimum(east, 0.0) - KAPPA
    pos_north = jnp.maximum(north, 0.0)
    neg_north = jnp.minimum(north, 0.0)
    new_flux = pos_east * q + neg_east * q_next
    cross = pos_north * q + neg_north * up_of(q)
    moved = q - (new_flux - flux) - (cross - down_of(cross))
    ahead = g_next - g
    new_drift = neg_east * ahead
    above = up_of(g) - g
    pulled = (
        g + (pos_east * ahead + drift) + (pos_north * above + down_of(neg_north * above))
    )
    return moved, pulled, new_flux, new_drift


def west_terms(q_prev, q, g_prev, g, east_prev):
    pos = jnp.maximum(east_prev, 0.0) + KAPPA
    neg = jnp.minimum(east_prev, 0.0) - KAPPA
    return pos * q_prev + neg * q, neg * (g - g_prev)


def first_kernel(
    start, blocks, state, state_prev, state_next, cot, cot_prev, cot_next, east, east_prev,
    north, low, high, first, back, cols, speeds, east_s, north_s, prev_s,
):
    here = lax.rem(pl.program_id(0) + start, blocks)
    flat = ROWS * 16
    east_s[...] = east[...].astype(F32).reshape(flat, 128)
    north_s[...] = north[...].astype(F32).reshape(flat, 128)
    prev_s[...] = east_prev[...].astype(F32).reshape(256, 128)
    q2 = state.reshape(flat, 128)
    g2 = cot.reshape(flat, 128)
    at_low = here == 0
    at_high = here == blocks - 1
    q_prev = jnp.where(at_low, low[0], rows_at(state_prev.reshape(128, 128), 7, 8))
    g_prev = jnp.where(at_low, low[1], rows_at(cot_prev.reshape(128, 128), 7, 8))
    e_prev = jnp.where(at_low, low[2], rows_at(prev_s, 15, 16))
    q_last = jnp.where(at_high, high[0], rows_at(state_next.reshape(128, 128), 0, 8))
    g_last = jnp.where(at_high, high[1], rows_at(cot_next.reshape(128, 128), 0, 8))
    q = rows_at(q2, 0, ROWS)
    g = rows_at(g2, 0, ROWS)
    flux, drift = west_terms(q_prev, q, g_prev, g, e_prev)

    def one(i, q, g, q_next, g_next, flux, drift):
        e = rows_at(east_s, i, ROWS)
        n = rows_at(north_s, i, ROWS)
        moved, pulled, flux, drift = step_row(q, q_next, g, g_next, e, n, flux, drift)
        first[i] = moved
        back[i] = pulled
        cols[i, 0] = moved.astype(BF16)
        cols[i, 1] = pulled.astype(BF16)
        speeds[i, 0] = e.astype(BF16)
        speeds[i, 1] = n.astype(BF16)
        return flux, drift

    for i in range(ROWS):
        if i < ROWS - 1:
            q_next = rows_at(q2, i + 1, ROWS)
            g_next = rows_at(g2, i + 1, ROWS)
        else:
            q_next, g_next = q_last, g_last
        flux, drift = one(i, q, g, q_next, g_next, flux, drift)
        q, g = q_next, g_next


def first_step(start, count, state, east, north, cot, low, high):
    width = state.shape[1]
    blocks = width // ROWS
    here = lambda s: lax.rem(s + start, blocks)
    before = lambda s, size: lax.rem(here(s) * (ROWS // size) - 1 + width // size, width // size)
    after = lambda s, size: lax.rem((here(s) + 1) * (ROWS // size), width // size)
    main = pl.BlockSpec((16, ROWS, 128), lambda s: (0, here(s), 0))
    prev = pl.BlockSpec((16, 8, 128), lambda s: (0, before(s, 8), 0))
    prev16 = pl.BlockSpec((16, 16, 128), lambda s: (0, before(s, 16), 0))
    post = pl.BlockSpec((16, 8, 128), lambda s: (0, after(s, 8), 0))
    whole = lambda n: pl.BlockSpec((n, 16, 128), lambda s: (0, 0, 0))
    rows = count * ROWS
    field = pl.BlockSpec((ROWS, 16, 128), lambda s: (s, 0, 0))
    pair = pl.BlockSpec((ROWS, 2, 16, 128), lambda s: (s, 0, 0, 0))
    return pl.pallas_call(
        functools.partial(first_kernel, start, blocks),
        grid=(count,),
        in_specs=[main, prev, post, main, prev, post, main, prev16, main, whole(3), whole(2)],
        out_specs=[field, field, pair, pair],
        out_shape=[
            jax.ShapeDtypeStruct((rows, 16, 128), F32),
            jax.ShapeDtypeStruct((rows, 16, 128), F32),
            jax.ShapeDtypeStruct((rows, 2, 16, 128), BF16),
            jax.ShapeDtypeStruct((rows, 2, 16, 128), BF16),
        ],
        scratch_shapes=[
            pltpu.VMEM((ROWS * 16, 128), F32),
            pltpu.VMEM((ROWS * 16, 128), F32),
            pltpu.VMEM((256, 128), F32),
        ],
        compiler_params=pltpu.CompilerParams(vmem_limit_bytes=VMEM_LIMIT),
        cost_estimate=pl.CostEstimate(
            flops=rows * 16 * 128 * 40, bytes_accessed=rows * 16 * 128 * 28, transcendentals=0
        ),
        name="transport_one",
    )(state, state, state, cot, cot, cot, east, east, north, low, high)


CELLS = 4
HTILE = 256


def network_kernel(cols, w_in_t, w_out_t, w_in, w_out, fields, grads, act_s, dpre_s):
    hidden = w_in_t.shape[0]

    @pl.when(pl.program_id(0) == 0)
    def _():
        grads[...] = jnp.zeros_like(grads)

    col = jnp.concatenate([cols[:, i, 0].reshape(128, 128) for i in range(CELLS)], 1)
    gcol = jnp.concatenate([cols[:, i, 1].reshape(128, 128) for i in range(CELLS)], 1)
    nt = (((1,), (1,)), ((), ()))
    for h in range(0, hidden, HTILE):
        part = slice(h, h + HTILE)
        z = jnp.dot(w_in_t[part, :], col, preferred_element_type=F32)
        z2 = z * z
        t = jnp.tanh(z * (z2 * (SLOPE_C * CUBIC) + SLOPE_C))
        half = 0.5 * t + 0.5
        slope = half + (1.0 - t * t) * (z * (z2 * (1.5 * SLOPE_C * CUBIC) + 0.5 * SLOPE_C))
        act = (z * half).astype(BF16)
        act_s[part, :] = act
        d_act = jnp.dot(w_out_t[part, :], gcol, preferred_element_type=F32)
        d_pre = (d_act * slope).astype(BF16)
        dpre_s[part, :] = d_pre
        grads[0, part, :] += lax.dot_general(d_pre, col, nt, preferred_element_type=F32)
        grads[1, part, :] += lax.dot_general(act, gcol, nt, preferred_element_type=F32)
    tend = jnp.dot(w_out[...], act_s[...], preferred_element_type=F32).astype(BF16)
    d_cols = jnp.dot(w_in[...], dpre_s[...], preferred_element_type=F32).astype(BF16)
    for i in range(CELLS):
        fields[:, i, 0] = tend[:, i * 128 : (i + 1) * 128].reshape(8, 16, 128)
        fields[:, i, 1] = d_cols[:, i * 128 : (i + 1) * 128].reshape(8, 16, 128)


def network(cols, w_in_t, w_out_t, w_in, w_out):
    rows = cols.shape[1]
    hidden = w_in.shape[1]
    block = pl.BlockSpec((8, CELLS, 2, 16, 128), lambda s: (0, s, 0, 0, 0))
    tall = pl.BlockSpec((hidden, 128), lambda s: (0, 0))
    wide = pl.BlockSpec((128, hidden), lambda s: (0, 0))
    return pl.pallas_call(
        network_kernel,
        grid=(rows // CELLS,),
        in_specs=[block, tall, tall, wide, wide],
        out_specs=[block, pl.BlockSpec((2, hidden, 128), lambda s: (0, 0, 0))],
        out_shape=[
            jax.ShapeDtypeStruct(cols.shape, BF16),
            jax.ShapeDtypeStruct((2, hidden, 128), F32),
        ],
        scratch_shapes=[
            pltpu.VMEM((hidden, CELLS * 128), BF16),
            pltpu.VMEM((hidden, CELLS * 128), BF16),
        ],
        compiler_params=pltpu.CompilerParams(vmem_limit_bytes=VMEM_LIMIT),
        cost_estimate=pl.CostEstimate(
            flops=rows * 128 * 128 * hidden * 12,
            bytes_accessed=rows * 128 * 128 * 8,
            transcendentals=rows * 128 * hidden,
        ),
        name="column_network",
    )(cols, w_in_t, w_out_t, w_in, w_out)


def last_kernel(
    first_a, back_a, speeds_a, fields_a, first_b, back_b, speeds_b, fields_b, low, high,
    out, grad,
):
    width = out.shape[1]
    half = width // 2
    quarter = width // 4
    out2 = out.reshape(16 * width, 128)
    grad2 = grad.reshape(16 * width, 128)
    inner = (first_a, back_a, speeds_a, fields_a)
    edges = (first_b, back_b, speeds_b, fields_b)

    def load(part, i):
        first, back, _, fields = part
        return (first[i] + fields[i, 0].astype(F32), back[i] + fields[i, 1].astype(F32))

    def segment(part, offset, place, size, q, g, flux, drift, ending):
        def one(i, carry, following):
            q, g, flux, drift = carry
            q_next, g_next = following
            e = part[2][offset + i, 0].astype(F32)
            n = part[2][offset + i, 1].astype(F32)
            moved, pulled, flux, drift = step_row(q, q_next, g, g_next, e, n, flux, drift)
            put_rows(out2, place + i, width, moved)
            put_rows(grad2, place + i, width, pulled)
            return q_next, g_next, flux, drift

        carry = lax.fori_loop(
            0,
            size - 1,
            lambda i, carry: one(i, carry, load(part, offset + i + 1)),
            (q, g, flux, drift),
            unroll=7,
        )
        return one(size - 1, carry, ending())

    q, g = load(edges, quarter)
    flux, drift = west_terms(low[0], q, low[1], g, low[2])
    carry = (q, g, flux, drift)
    carry = segment(edges, quarter, 0, quarter, *carry, lambda: load(inner, 0))
    carry = segment(inner, 0, quarter, half, *carry, lambda: load(edges, 0))
    segment(edges, 0, quarter + half, quarter, *carry, lambda: (high[0], high[1]))


def last_step(parts, low, high, shape):
    spec = pl.BlockSpec(memory_space=pltpu.VMEM)
    return pl.pallas_call(
        last_kernel,
        in_specs=[spec] * 10,
        out_specs=[spec] * 2,
        out_shape=[jax.ShapeDtypeStruct(shape, F32)] * 2,
        compiler_params=pltpu.CompilerParams(vmem_limit_bytes=VMEM_LIMIT),
        cost_estimate=pl.CostEstimate(
            flops=shape[0] * shape[1] * shape[2] * 40,
            bytes_accessed=shape[0] * shape[1] * shape[2] * 24,
            transcendentals=0,
        ),
        name="transport_two",
    )(*parts, low, high)


def shift(block, distance):
    count = lax.axis_size("tile")
    return lax.ppermute(block, "tile", [(i, (i + distance) % count) for i in range(count)])


def exchange(block):
    return lax.all_to_all(block, "lev", split_axis=0, concat_axis=0, tiled=True)


def partner(block, mask):
    return lax.ppermute(block, "tile", [(i, i ^ mask) for i in range(lax.axis_size("tile"))])


def total_of(grads):
    core = lax.rem(lax.axis_index("tile"), 2)
    mine = lax.dynamic_index_in_dim(grads, core, 0, False)
    other = lax.dynamic_index_in_dim(grads, 1 - core, 0, False)
    part = mine + partner(other, 1)
    hidden = part.shape[0]
    part = jnp.sum(exchange(part.reshape(8, hidden // 8, 128)), 0)
    for base in (2, 8):
        one, two, three = (partner(part, base * k) for k in (1, 2, 3))
        part = (part + one) + (two + three)
    part = exchange(jnp.broadcast_to(part[None], (8, hidden // 8, 128))).reshape(hidden, 128)
    other = partner(part, 1)
    return jnp.where(core == 0, part, other), jnp.where(core == 0, other, part)


def shards(state_in, east_speed, north_speed, w_in, w_out, cotangent):
    width = state_in.shape[1]
    blocks = width // ROWS
    low = shift(
        jnp.stack([state_in[:, -1], cotangent[:, -1], east_speed[:, -1].astype(F32)]), 1
    )
    high = shift(jnp.stack([state_in[:, 0], cotangent[:, 0]]), -1)
    w_in_t, w_out_t = w_in.T, w_out.T
    results = []
    grads = 0.0
    none = jnp.zeros((3, 16, 128), F32)
    for start, lo, hi in ((blocks // 4, none, none[:2]), (3 * blocks // 4, low, high)):
        first, back, cols, speeds = first_step(
            start, blocks // 2, state_in, east_speed, north_speed, cotangent, lo, hi
        )
        rows = cols.shape[0] // 8
        got = exchange(cols.reshape(8, rows, 2, 16, 128))
        fields, part = network(got, w_in_t, w_out_t, w_in, w_out)
        grads = grads + part
        fields = exchange(fields).reshape(8 * rows, 2, 16, 128)
        results.append((first, back, speeds, fields))
    first, back, speeds, fields = results[1]
    quarter = width // 4

    def edge(i):
        return first[i] + fields[i, 0].astype(F32), back[i] + fields[i, 1].astype(F32)

    second_low = shift(jnp.stack(edge(quarter - 1)), 1)
    second_high = shift(jnp.stack(edge(quarter)), -1)
    lows = jnp.concatenate([second_low, low[2:]])
    state_out, state_grad = last_step(
        results[0] + results[1], lows, second_high, state_in.shape
    )
    in_total, out_total = total_of(grads)
    scale = 1.0 / math.sqrt(lax.axis_size("tile") * width * state_in.shape[2])
    return state_out, state_grad, in_total.T * scale, out_total.T * scale


def solution(mesh):
    field = P("lev", "tile", None)
    return jax.shard_map(
        shards,
        mesh=mesh,
        in_specs=(field, field, field, P(), P(), field),
        out_specs=(field, field, P(), P()),
        check_vma=False,
    )
```

```python
import functools
import math

import jax
import jax.numpy as jnp
from jax import lax
from jax.experimental import pallas as pl
from jax.experimental.pallas import tpu as pltpu
from jax.sharding import PartitionSpec as P

KAPPA = 0.05
SLOPE_C = 0.7978845608028654
CUBIC = 0.044715
ROWS = 32
UNROLL = 16
F32 = jnp.float32
BF16 = jnp.bfloat16
MIB = 1024 * 1024


def spread(pairs, tile):
    for ref, scratch in pairs:
        size = min(16, ref.shape[1])
        place = pl.multiple_of(tile * 16, size)
        part = ref[:, pl.ds(place, size), :].astype(F32)
        part = jnp.swapaxes(part, 0, 1).reshape(size * 16, 128)
        scratch[pl.ds(pl.multiple_of(tile * 256, 256), size * 16), :] = part


def row(ref, index):
    return ref[pl.ds(pl.multiple_of(index * 16, 16), 16), :]


def put_rows(ref, index, stride, value):
    ref[pl.ds(index, 8, stride), :] = value[:8]
    ref[pl.ds(index + 8 * stride, 8, stride), :] = value[8:]


def up_of(value):
    return pltpu.roll(value, value.shape[1] - 1, 1)


def down_of(value):
    return pltpu.roll(value, 1, 1)


def wall_mask(north):
    lane = lax.broadcasted_iota(jnp.int32, north.shape, 1)
    return jnp.where(lane < north.shape[1] - 1, north, 0.0)


def step_row(q, q_next, g, g_next, east, north, flux, drift):
    north = wall_mask(north)
    pos_east = jnp.maximum(east, 0.0) + KAPPA
    neg_east = jnp.minimum(east, 0.0) - KAPPA
    pos_north = jnp.maximum(north, 0.0)
    neg_north = jnp.minimum(north, 0.0)
    new_flux = pos_east * q + neg_east * q_next
    cross = pos_north * q + neg_north * up_of(q)
    moved = q - (new_flux - flux) - (cross - down_of(cross))
    ahead = g_next - g
    new_drift = neg_east * ahead
    above = up_of(g) - g
    pulled = (
        g + (pos_east * ahead + drift) + (pos_north * above + down_of(neg_north * above))
    )
    return moved, pulled, new_flux, new_drift


def west_terms(q_prev, q, g_prev, g, east_prev):
    pos = jnp.maximum(east_prev, 0.0) + KAPPA
    neg = jnp.minimum(east_prev, 0.0) - KAPPA
    return pos * q_prev + neg * q, neg * (g - g_prev)


def first_kernel(
    start, blocks, state, state_prev, state_next, cot, cot_prev, cot_next, east, east_prev,
    north, low, high, *rest,
):
    first, back, speeds, cols, q_s, g_s, east_s, north_s = rest[-13:-5]
    prev_s, gprev_s, next_s, gnext_s, eprev_s = rest[-5:]
    here = lax.rem(pl.program_id(0) + start, blocks)
    at_low = here == 0
    at_high = here == blocks - 1
    pairs = ((state, q_s), (cot, g_s), (east, east_s), (north, north_s))

    def spread_tile(tile, carry):
        spread(pairs, tile)
        return carry

    lax.fori_loop(0, ROWS // 16, spread_tile, 0)
    spread(((state_prev, prev_s), (cot_prev, gprev_s), (east_prev, eprev_s)), 0)
    spread(((state_next, next_s), (cot_next, gnext_s)), 0)
    q_prev = jnp.where(at_low, low[0], row(prev_s, 7))
    g_prev = jnp.where(at_low, low[1], row(gprev_s, 7))
    e_prev = jnp.where(at_low, low[2], row(eprev_s, 15))
    q_s[ROWS * 16 :, :] = jnp.where(at_high, high[0], row(next_s, 0))
    g_s[ROWS * 16 :, :] = jnp.where(at_high, high[1], row(gnext_s, 0))
    q = row(q_s, 0)
    g = row(g_s, 0)
    flux, drift = west_terms(q_prev, q, g_prev, g, e_prev)

    def one(i, carry):
        q, g, flux, drift = carry
        q_next = row(q_s, i + 1)
        g_next = row(g_s, i + 1)
        e = row(east_s, i)
        n = row(north_s, i)
        moved, pulled, flux, drift = step_row(q, q_next, g, g_next, e, n, flux, drift)
        first[i] = moved
        back[i] = pulled
        cols[i, 0] = moved.astype(BF16)
        cols[i, 1] = pulled.astype(BF16)
        speeds[i, 0] = e.astype(BF16)
        speeds[i, 1] = n.astype(BF16)
        return q_next, g_next, flux, drift

    lax.fori_loop(0, ROWS, one, (q, g, flux, drift), unroll=UNROLL)


def in_hbm(array):
    return pltpu.with_memory_space_constraint(array, pltpu.HBM)


def first_step(start, count, state, east, north, cot, low, high, filled):
    width = state.shape[1]
    blocks = width // ROWS
    here = lambda s: lax.rem(s + start, blocks)
    before = lambda s, size: lax.rem(here(s) * (ROWS // size) - 1 + width // size, width // size)
    after = lambda s, size: lax.rem((here(s) + 1) * (ROWS // size), width // size)
    main = pl.BlockSpec((16, ROWS, 128), lambda s: (0, here(s), 0))
    prev = pl.BlockSpec((16, 8, 128), lambda s: (0, before(s, 8), 0))
    prev16 = pl.BlockSpec((16, 16, 128), lambda s: (0, before(s, 16), 0))
    post = pl.BlockSpec((16, 8, 128), lambda s: (0, after(s, 8), 0))
    whole = lambda n: pl.BlockSpec((n, 16, 128), lambda s: (0, 0, 0))
    rows = count * ROWS
    field = pl.BlockSpec((ROWS, 16, 128), lambda s: (here(s), 0, 0))
    speed = pl.BlockSpec((ROWS, 2, 16, 128), lambda s: (here(s), 0, 0, 0))
    pair = pl.BlockSpec((ROWS, 2, 16, 128), lambda s: (s, 0, 0, 0))
    return pl.pallas_call(
        functools.partial(first_kernel, start, blocks),
        grid=(count,),
        in_specs=[main, prev, post, main, prev, post, main, prev16, main, whole(3), whole(2)]
        + [pl.BlockSpec(memory_space=pl.ANY)] * len(filled),
        out_specs=[field, field, speed, pair],
        out_shape=[
            pltpu.HBM((width, 16, 128), F32),
            pltpu.HBM((width, 16, 128), F32),
            pltpu.HBM((width, 2, 16, 128), BF16),
            pltpu.HBM((rows, 2, 16, 128), BF16),
        ],
        input_output_aliases={11 + k: k for k in range(len(filled))},
        scratch_shapes=[
            pltpu.VMEM(((ROWS + 1) * 16, 128), F32),
            pltpu.VMEM(((ROWS + 1) * 16, 128), F32),
            pltpu.VMEM((ROWS * 16, 128), F32),
            pltpu.VMEM((ROWS * 16, 128), F32),
            pltpu.VMEM((128, 128), F32),
            pltpu.VMEM((128, 128), F32),
            pltpu.VMEM((128, 128), F32),
            pltpu.VMEM((128, 128), F32),
            pltpu.VMEM((256, 128), F32),
        ],
        compiler_params=pltpu.CompilerParams(vmem_limit_bytes=16 * MIB),
        cost_estimate=pl.CostEstimate(
            flops=rows * 16 * 128 * 40, bytes_accessed=rows * 16 * 128 * 28, transcendentals=0
        ),
        name="transport_one",
    )(
        *[in_hbm(x) for x in (state, state, state, cot, cot, cot, east, east, north)],
        low,
        high,
        *filled,
    )


def edge_kernel(state_lo, state_hi, cot_lo, cot_hi, east_hi, low, high):
    low[0] = state_hi[:, 7, :]
    low[1] = cot_hi[:, 7, :]
    low[2] = east_hi[...].astype(F32)[:, 15, :]
    high[0] = state_lo[:, 0, :]
    high[1] = cot_lo[:, 0, :]


def edge_rows(state, east, cot):
    width = state.shape[1]
    head = pl.BlockSpec((16, 8, 128), lambda s: (0, 0, 0))
    tail = pl.BlockSpec((16, 8, 128), lambda s: (0, width // 8 - 1, 0))
    tail16 = pl.BlockSpec((16, 16, 128), lambda s: (0, width // 16 - 1, 0))
    return pl.pallas_call(
        edge_kernel,
        grid=(1,),
        in_specs=[head, tail, head, tail, tail16],
        out_specs=[
            pl.BlockSpec((3, 16, 128), lambda s: (0, 0, 0)),
            pl.BlockSpec((2, 16, 128), lambda s: (0, 0, 0)),
        ],
        out_shape=[
            jax.ShapeDtypeStruct((3, 16, 128), F32),
            jax.ShapeDtypeStruct((2, 16, 128), F32),
        ],
        name="edge_rows",
    )(*[in_hbm(x) for x in (state, state, cot, cot, east)])


CELLS = 8
HTILE = 256


def network_kernel(cols, w_in_t, w_out_t, w_in, w_out, before, fields, grads, act_s, dpre_s):
    hidden = w_in_t.shape[0]

    @pl.when(pl.program_id(0) == 0)
    def _():
        grads[...] = before[...]

    col = jnp.concatenate([cols[:, i, 0].reshape(128, 128) for i in range(CELLS)], 1)
    gcol = jnp.concatenate([cols[:, i, 1].reshape(128, 128) for i in range(CELLS)], 1)
    nt = (((1,), (1,)), ((), ()))
    for h in range(0, hidden, HTILE):
        part = slice(h, h + HTILE)
        z = jnp.dot(w_in_t[part, :], col, preferred_element_type=F32)
        z2 = z * z
        t = jnp.tanh(z * (z2 * (SLOPE_C * CUBIC) + SLOPE_C))
        half = 0.5 * t + 0.5
        slope = half + (1.0 - t * t) * (z * (z2 * (1.5 * SLOPE_C * CUBIC) + 0.5 * SLOPE_C))
        act = (z * half).astype(BF16)
        act_s[part, :] = act
        d_act = jnp.dot(w_out_t[part, :], gcol, preferred_element_type=F32)
        d_pre = (d_act * slope).astype(BF16)
        dpre_s[part, :] = d_pre
        grads[0, part, :] += lax.dot_general(d_pre, col, nt, preferred_element_type=F32)
        grads[1, part, :] += lax.dot_general(act, gcol, nt, preferred_element_type=F32)
    tend = jnp.dot(w_out[...], act_s[...], preferred_element_type=F32).astype(BF16)
    d_cols = jnp.dot(w_in[...], dpre_s[...], preferred_element_type=F32).astype(BF16)
    for i in range(CELLS):
        fields[:, i, 0] = tend[:, i * 128 : (i + 1) * 128].reshape(8, 16, 128)
        fields[:, i, 1] = d_cols[:, i * 128 : (i + 1) * 128].reshape(8, 16, 128)


def network(cols, w_in_t, w_out_t, w_in, w_out, grads):
    rows = cols.shape[1]
    hidden = w_in.shape[1]
    block = pl.BlockSpec((8, CELLS, 2, 16, 128), lambda s: (0, s, 0, 0, 0))
    tall = pl.BlockSpec((hidden, 128), lambda s: (0, 0))
    wide = pl.BlockSpec((128, hidden), lambda s: (0, 0))
    total = pl.BlockSpec((2, hidden, 128), lambda s: (0, 0, 0))
    return pl.pallas_call(
        functools.partial(network_kernel),
        grid=(rows // CELLS,),
        in_specs=[block, tall, tall, wide, wide, total],
        out_specs=[block, total],
        out_shape=[
            pltpu.HBM(cols.shape, BF16),
            jax.ShapeDtypeStruct((2, hidden, 128), F32),
        ],
        scratch_shapes=[
            pltpu.VMEM((hidden, CELLS * 128), BF16),
            pltpu.VMEM((hidden, CELLS * 128), BF16),
        ],
        compiler_params=pltpu.CompilerParams(vmem_limit_bytes=24 * MIB),
        cost_estimate=pl.CostEstimate(
            flops=rows * 128 * 128 * hidden * 12,
            bytes_accessed=rows * 128 * 128 * 8,
            transcendentals=rows * 128 * hidden,
        ),
        name="column_network",
    )(in_hbm(cols), w_in_t, w_out_t, w_in, w_out, grads)


def last_kernel(
    first, first_next, back, back_next, speeds, inner, inner_next, outer, outer_next, low, high,
    out, grad, q_s, g_s, flux_s, drift_s,
):
    here = pl.program_id(0)
    blocks = pl.num_programs(0)
    inside = jnp.logical_and(here >= blocks // 4, here < blocks - blocks // 4)

    def fill(fields):
        def one(i, carry):
            at = pl.ds(pl.multiple_of(i * 16, 16), 16)
            q_s[at, :] = first[i] + fields[i, 0].astype(F32)
            g_s[at, :] = back[i] + fields[i, 1].astype(F32)
            return carry

        lax.fori_loop(0, ROWS, one, 0, unroll=UNROLL)

    pl.when(inside)(lambda: fill(inner))
    pl.when(jnp.logical_not(inside))(lambda: fill(outer))
    last = here == blocks - 1
    next_inside = jnp.logical_and(here + 1 >= blocks // 4, here + 1 < blocks - blocks // 4)
    add = jnp.where(next_inside, inner_next[0].astype(F32), outer_next[0].astype(F32))
    q_s[ROWS * 16 :, :] = jnp.where(last, high[0], first_next[0] + add[0])
    g_s[ROWS * 16 :, :] = jnp.where(last, high[1], back_next[0] + add[1])
    q = row(q_s, 0)
    g = row(g_s, 0)
    flux, drift = west_terms(low[0], q, low[1], g, low[2])
    flux = jnp.where(here == 0, flux, flux_s[...])
    drift = jnp.where(here == 0, drift, drift_s[...])
    out2 = out.reshape(16 * ROWS, 128)
    grad2 = grad.reshape(16 * ROWS, 128)

    def one(i, carry):
        q, g, flux, drift = carry
        q_next = row(q_s, i + 1)
        g_next = row(g_s, i + 1)
        e = speeds[i, 0].astype(F32)
        n = speeds[i, 1].astype(F32)
        moved, pulled, flux, drift = step_row(q, q_next, g, g_next, e, n, flux, drift)
        put_rows(out2, i, ROWS, moved)
        put_rows(grad2, i, ROWS, pulled)
        return q_next, g_next, flux, drift

    carry = lax.fori_loop(0, ROWS, one, (q, g, flux, drift), unroll=UNROLL)
    flux_s[...] = carry[2]
    drift_s[...] = carry[3]


def last_step(first, back, speeds, inner, outer, low, high, shape):
    width = shape[1]
    blocks = width // ROWS
    part = blocks // 4
    quarter = width // 4
    held = lambda s: jnp.clip(s - part, 0, 2 * part - 1)
    kept = lambda s: jnp.where(s < 3 * part, jnp.minimum(s + part, 2 * part - 1), s - 3 * part)
    row_held = lambda r: jnp.clip(r - quarter, 0, 2 * quarter - 1)
    row_kept = lambda r: jnp.where(
        r < quarter, r + quarter, jnp.clip(r - 3 * quarter, 0, 2 * quarter - 1)
    )
    after = lambda s: jnp.minimum((s + 1) * ROWS, width - 1)
    field = pl.BlockSpec((ROWS, 16, 128), lambda s: (s, 0, 0))
    field_next = pl.BlockSpec((1, 16, 128), lambda s: (after(s), 0, 0))
    pair = lambda index: pl.BlockSpec((ROWS, 2, 16, 128), lambda s: (index(s), 0, 0, 0))
    pair_next = lambda index: pl.BlockSpec(
        (1, 2, 16, 128), lambda s: (index((s + 1) * ROWS), 0, 0, 0)
    )
    whole = lambda n: pl.BlockSpec((n, 16, 128), lambda s: (0, 0, 0))
    result = pl.BlockSpec((16, ROWS, 128), lambda s: (0, s, 0))
    return pl.pallas_call(
        last_kernel,
        grid=(blocks,),
        in_specs=[
            field, field_next, field, field_next, pair(lambda s: s),
            pair(held), pair_next(row_held), pair(kept), pair_next(row_kept), whole(3), whole(2),
        ],
        out_specs=[result] * 2,
        out_shape=[pltpu.HBM(shape, F32)] * 2,
        scratch_shapes=[pltpu.VMEM(((ROWS + 1) * 16, 128), F32)] * 2
        + [pltpu.VMEM((16, 128), F32)] * 2,
        compiler_params=pltpu.CompilerParams(vmem_limit_bytes=16 * MIB),
        cost_estimate=pl.CostEstimate(
            flops=shape[0] * shape[1] * shape[2] * 40,
            bytes_accessed=shape[0] * shape[1] * shape[2] * 24,
            transcendentals=0,
        ),
        name="transport_two",
    )(*[in_hbm(x) for x in (first, first, back, back, speeds, inner, inner, outer, outer)], low, high)


def shift(block, distance):
    count = lax.axis_size("tile")
    return lax.ppermute(block, "tile", [(i, (i + distance) % count) for i in range(count)])


def exchange(block):
    return lax.all_to_all(block, "lev", split_axis=0, concat_axis=0, tiled=True)


def partner(block, mask):
    return lax.ppermute(block, "tile", [(i, i ^ mask) for i in range(lax.axis_size("tile"))])


def chip_sum(grads):
    core = lax.rem(lax.axis_index("tile"), 2)
    mine = lax.dynamic_index_in_dim(grads, core, 0, False)
    other = lax.dynamic_index_in_dim(grads, 1 - core, 0, False)
    return mine + partner(other, 1)


def exchange_rows(block):
    lev = lax.axis_size("lev")
    groups = [
        [(y * 8 + rest) * lev + k for y in range(4) for k in range(lev)] for rest in range(8)
    ]
    return lax.all_to_all(
        block, ("tile", "lev"), split_axis=0, concat_axis=0, tiled=True, axis_index_groups=groups
    )


def z_sum(part):
    one, two, three = (partner(part, 2 * k) for k in (1, 2, 3))
    return (part + one) + (two + three)


def shards(state_in, east_speed, north_speed, w_in, w_out, cotangent):
    width = state_in.shape[1]
    blocks = width // ROWS
    hidden = w_in.shape[1]
    barrier = lax.optimization_barrier
    low, high = edge_rows(state_in, east_speed, cotangent)
    low, high, state_in = barrier((low, high, state_in))
    low = shift(low, 1)
    high = shift(high, -1)
    w_in_t, w_out_t = w_in.T, w_out.T
    none = jnp.zeros((3, 16, 128), F32)
    half = blocks // 2
    fields_in = (state_in, east_speed, north_speed, cotangent)
    *held, cols_a = first_step(blocks // 4, half, *fields_in, none, none[:2], ())
    cols_a, low, high = barrier((cols_a, low, high))
    got_a = exchange(cols_a.reshape(8, width // 16, 2, 16, 128))
    first, back, speeds, cols_b = first_step(3 * blocks // 4, half, *fields_in, low, high, held)
    got_b = exchange(cols_b.reshape(8, width // 16, 2, 16, 128))
    zero = jnp.zeros((2, hidden, 128), F32)
    fields_a, grads = network(got_a, w_in_t, w_out_t, w_in, w_out, zero)
    fields_a = exchange(fields_a)
    fields_b, grads = network(got_b, w_in_t, w_out_t, w_in, w_out, grads)
    grads, fields_a = barrier((grads, fields_a))
    part = chip_sum(grads)
    part = jnp.sum(exchange_rows(part.reshape(32, hidden // 32, 128)), 0)
    part, fields_b = barrier((part, fields_b))
    fields_b = exchange(fields_b)
    part = z_sum(part)
    part, fields_b = barrier((part, fields_b))
    inner = fields_a.reshape(width // 2, 2, 16, 128)
    outer = fields_b.reshape(width // 2, 2, 16, 128)
    quarter = width // 4

    def edge(row, i):
        return jnp.stack([first[row], back[row]]) + outer[i].astype(F32)

    second_low = shift(edge(width - 1, quarter - 1), 1)
    second_high = shift(edge(0, quarter), -1)
    lows = jnp.concatenate([second_low, low[2:]])
    part = exchange_rows(jnp.broadcast_to(part[None], (32,) + part.shape)).reshape(hidden, 128)
    state_out, state_grad = last_step(
        first, back, speeds, inner, outer, lows, second_high, state_in.shape
    )
    part, state_out, state_grad = barrier((part, state_out, state_grad))
    other = partner(part, 1)
    core = lax.rem(lax.axis_index("tile"), 2)
    in_total = jnp.where(core == 0, part, other)
    out_total = jnp.where(core == 0, other, part)
    scale = 1.0 / math.sqrt(lax.axis_size("tile") * width * state_in.shape[2])
    return state_out, state_grad, in_total.T * scale, out_total.T * scale


def solution(mesh):
    field = P("lev", "tile", None)
    return jax.shard_map(
        shards,
        mesh=mesh,
        in_specs=(field, field, field, P(), P(), field),
        out_specs=(field, field, P(), P()),
        check_vma=False,
    )
```

```python
import functools
import math

import jax
import jax.numpy as jnp
from jax import lax
from jax.experimental import pallas as pl
from jax.experimental.pallas import tpu as pltpu
from jax.sharding import PartitionSpec as P

KAPPA = 0.05
SLOPE_C = 0.7978845608028654
CUBIC = 0.044715
ROWS = 64
LAST_ROWS = 32
SUB = 256
UNROLL = 16
SAMPLES = 8192 * 128
F32 = jnp.float32
BF16 = jnp.bfloat16
MIB = 1024 * 1024


def spread(pairs, tile):
    for ref, scratch in pairs:
        size = min(16, ref.shape[1])
        place = pl.multiple_of(tile * 16, size)
        part = ref[:, pl.ds(place, size), :].astype(F32)
        part = jnp.swapaxes(part, 0, 1).reshape(size * 16, 128)
        scratch[pl.ds(pl.multiple_of(tile * 256, 256), size * 16), :] = part


def row(ref, index):
    return ref[pl.ds(pl.multiple_of(index * 16, 16), 16), :]


def put_rows(ref, index, stride, value):
    ref[pl.ds(index, 8, stride), :] = value[:8]
    ref[pl.ds(index + 8 * stride, 8, stride), :] = value[8:]


def up_of(value):
    return pltpu.roll(value, value.shape[1] - 1, 1)


def down_of(value):
    return pltpu.roll(value, 1, 1)


def wall_mask(north):
    lane = lax.broadcasted_iota(jnp.int32, north.shape, 1)
    return jnp.where(lane < north.shape[1] - 1, north, 0.0)


def step_row(q, q_next, g, g_next, east, north, flux, drift):
    north = wall_mask(north)
    pos_east = jnp.maximum(east, 0.0) + KAPPA
    neg_east = jnp.minimum(east, 0.0) - KAPPA
    pos_north = jnp.maximum(north, 0.0)
    neg_north = jnp.minimum(north, 0.0)
    new_flux = pos_east * q + neg_east * q_next
    cross = pos_north * q + neg_north * up_of(q)
    moved = q - (new_flux - flux) - (cross - down_of(cross))
    ahead = g_next - g
    new_drift = neg_east * ahead
    above = up_of(g) - g
    pulled = (
        g + (pos_east * ahead + drift) + (pos_north * above + down_of(neg_north * above))
    )
    return moved, pulled, new_flux, new_drift


def west_terms(q_prev, q, g_prev, g, east_prev):
    pos = jnp.maximum(east_prev, 0.0) + KAPPA
    neg = jnp.minimum(east_prev, 0.0) - KAPPA
    return pos * q_prev + neg * q, neg * (g - g_prev)


def first_kernel(
    start, blocks, state, state_prev, state_next, cot, cot_prev, cot_next, east, east_prev,
    north, low, high, *rest,
):
    first, back, speeds, cols, q_s, g_s, east_s, north_s = rest[-13:-5]
    prev_s, gprev_s, next_s, gnext_s, eprev_s = rest[-5:]
    here = lax.rem(pl.program_id(0) + start, blocks)
    at_low = here == 0
    at_high = here == blocks - 1
    pairs = ((state, q_s), (cot, g_s), (east, east_s), (north, north_s))

    def spread_tile(tile, carry):
        spread(pairs, tile)
        return carry

    lax.fori_loop(0, ROWS // 16, spread_tile, 0)
    spread(((state_prev, prev_s), (cot_prev, gprev_s), (east_prev, eprev_s)), 0)
    spread(((state_next, next_s), (cot_next, gnext_s)), 0)
    q_prev = jnp.where(at_low, low[0], row(prev_s, 7))
    g_prev = jnp.where(at_low, low[1], row(gprev_s, 7))
    e_prev = jnp.where(at_low, low[2], row(eprev_s, 15))
    q_s[ROWS * 16 :, :] = jnp.where(at_high, high[0], row(next_s, 0))
    g_s[ROWS * 16 :, :] = jnp.where(at_high, high[1], row(gnext_s, 0))
    q = row(q_s, 0)
    g = row(g_s, 0)
    flux, drift = west_terms(q_prev, q, g_prev, g, e_prev)

    def one(i, carry):
        q, g, flux, drift = carry
        q_next = row(q_s, i + 1)
        g_next = row(g_s, i + 1)
        e = row(east_s, i)
        n = row(north_s, i)
        moved, pulled, flux, drift = step_row(q, q_next, g, g_next, e, n, flux, drift)
        first[i] = moved
        back[i] = pulled
        cols[i, 0] = moved.astype(BF16)
        cols[i, 1] = pulled.astype(BF16)
        speeds[i, 0] = e.astype(BF16)
        speeds[i, 1] = n.astype(BF16)
        return q_next, g_next, flux, drift

    lax.fori_loop(0, ROWS, one, (q, g, flux, drift), unroll=UNROLL)


def in_hbm(array):
    return pltpu.with_memory_space_constraint(array, pltpu.HBM)


def first_step(start, count, state, east, north, cot, low, high, filled):
    width = state.shape[1]
    blocks = width // ROWS
    here = lambda s: lax.rem(s + start, blocks)
    before = lambda s, size: lax.rem(here(s) * (ROWS // size) - 1 + width // size, width // size)
    after = lambda s, size: lax.rem((here(s) + 1) * (ROWS // size), width // size)
    main = pl.BlockSpec((16, ROWS, 128), lambda s: (0, here(s), 0))
    prev = pl.BlockSpec((16, 8, 128), lambda s: (0, before(s, 8), 0))
    prev16 = pl.BlockSpec((16, 16, 128), lambda s: (0, before(s, 16), 0))
    post = pl.BlockSpec((16, 8, 128), lambda s: (0, after(s, 8), 0))
    whole = lambda n: pl.BlockSpec((n, 16, 128), lambda s: (0, 0, 0))
    rows = count * ROWS
    field = pl.BlockSpec((ROWS, 16, 128), lambda s: (here(s), 0, 0))
    speed = pl.BlockSpec((ROWS, 2, 16, 128), lambda s: (here(s), 0, 0, 0))
    pair = pl.BlockSpec((ROWS, 2, 16, 128), lambda s: (s, 0, 0, 0))
    return pl.pallas_call(
        functools.partial(first_kernel, start, blocks),
        grid=(count,),
        in_specs=[main, prev, post, main, prev, post, main, prev16, main, whole(3), whole(2)]
        + [pl.BlockSpec(memory_space=pl.ANY)] * len(filled),
        out_specs=[field, field, speed, pair],
        out_shape=[
            pltpu.HBM((width, 16, 128), F32),
            pltpu.HBM((width, 16, 128), F32),
            pltpu.HBM((width, 2, 16, 128), BF16),
            pltpu.HBM((rows, 2, 16, 128), BF16),
        ],
        input_output_aliases={11 + k: k for k in range(len(filled))},
        scratch_shapes=[
            pltpu.VMEM(((ROWS + 1) * 16, 128), F32),
            pltpu.VMEM(((ROWS + 1) * 16, 128), F32),
            pltpu.VMEM((ROWS * 16, 128), F32),
            pltpu.VMEM((ROWS * 16, 128), F32),
            pltpu.VMEM((128, 128), F32),
            pltpu.VMEM((128, 128), F32),
            pltpu.VMEM((128, 128), F32),
            pltpu.VMEM((128, 128), F32),
            pltpu.VMEM((256, 128), F32),
        ],
        compiler_params=pltpu.CompilerParams(vmem_limit_bytes=16 * MIB),
        cost_estimate=pl.CostEstimate(
            flops=rows * 16 * 128 * 40, bytes_accessed=rows * 16 * 128 * 28, transcendentals=0
        ),
        name="transport_one",
    )(
        *[in_hbm(x) for x in (state, state, state, cot, cot, cot, east, east, north)],
        low,
        high,
        *filled,
    )


def edge_kernel(state_lo, state_hi, cot_lo, cot_hi, east_hi, low, high):
    low[0] = state_hi[:, 7, :]
    low[1] = cot_hi[:, 7, :]
    low[2] = east_hi[...].astype(F32)[:, 15, :]
    high[0] = state_lo[:, 0, :]
    high[1] = cot_lo[:, 0, :]


def edge_rows(state, east, cot):
    width = state.shape[1]
    head = pl.BlockSpec((16, 8, 128), lambda s: (0, 0, 0))
    tail = pl.BlockSpec((16, 8, 128), lambda s: (0, width // 8 - 1, 0))
    tail16 = pl.BlockSpec((16, 16, 128), lambda s: (0, width // 16 - 1, 0))
    return pl.pallas_call(
        edge_kernel,
        grid=(1,),
        in_specs=[head, tail, head, tail, tail16],
        out_specs=[
            pl.BlockSpec((3, 16, 128), lambda s: (0, 0, 0)),
            pl.BlockSpec((2, 16, 128), lambda s: (0, 0, 0)),
        ],
        out_shape=[
            jax.ShapeDtypeStruct((3, 16, 128), F32),
            jax.ShapeDtypeStruct((2, 16, 128), F32),
        ],
        name="edge_rows",
    )(*[in_hbm(x) for x in (state, state, cot, cot, east)])


CELLS = 8
HTILE = 256


def network_kernel(cols, w_in_t, w_out_t, w_in, w_out, before, fields, grads, act_s, dpre_s):
    hidden = w_in_t.shape[0]

    @pl.when(pl.program_id(0) == 0)
    def _():
        grads[...] = before[...]

    col = jnp.concatenate([cols[:, i, 0].reshape(128, 128) for i in range(CELLS)], 1)
    gcol = jnp.concatenate([cols[:, i, 1].reshape(128, 128) for i in range(CELLS)], 1)
    for h in range(0, hidden, HTILE):
        part = slice(h, h + HTILE)
        for n in range(0, CELLS * 128, SUB):
            at = slice(n, n + SUB)
            z = jnp.dot(w_in_t[part, :], col[:, at], preferred_element_type=F32)
            d_act = jnp.dot(w_out_t[part, :], gcol[:, at], preferred_element_type=F32)
            z2 = z * z
            t = jnp.tanh(z * (z2 * (SLOPE_C * CUBIC) + SLOPE_C))
            part_t = 0.5 * t
            half = part_t + 0.5
            act = z * half
            slope = half + act * (0.5 - part_t) * (
                z2 * (6.0 * SLOPE_C * CUBIC) + 2.0 * SLOPE_C
            )
            act_s[part, at] = act.astype(BF16)
            dpre_s[part, at] = (d_act * slope).astype(BF16)
    nt = (((1,), (1,)), ((), ()))
    grads[0] += lax.dot_general(dpre_s[...], col, nt, preferred_element_type=F32)
    grads[1] += lax.dot_general(act_s[...], gcol, nt, preferred_element_type=F32)
    tend = jnp.dot(w_out[...], act_s[...], preferred_element_type=F32).astype(BF16)
    d_cols = jnp.dot(w_in[...], dpre_s[...], preferred_element_type=F32).astype(BF16)
    for i in range(CELLS):
        fields[:, i, 0] = tend[:, i * 128 : (i + 1) * 128].reshape(8, 16, 128)
        fields[:, i, 1] = d_cols[:, i * 128 : (i + 1) * 128].reshape(8, 16, 128)


def network(cols, w_in_t, w_out_t, w_in, w_out, grads):
    rows = cols.shape[1]
    hidden = w_in.shape[1]
    block = pl.BlockSpec((8, CELLS, 2, 16, 128), lambda s: (0, s, 0, 0, 0))
    tall = pl.BlockSpec((hidden, 128), lambda s: (0, 0))
    wide = pl.BlockSpec((128, hidden), lambda s: (0, 0))
    total = pl.BlockSpec((2, hidden, 128), lambda s: (0, 0, 0))
    return pl.pallas_call(
        functools.partial(network_kernel),
        grid=(rows // CELLS,),
        in_specs=[block, tall, tall, wide, wide, total],
        out_specs=[block, total],
        out_shape=[
            pltpu.HBM(cols.shape, BF16),
            jax.ShapeDtypeStruct((2, hidden, 128), F32),
        ],
        scratch_shapes=[
            pltpu.VMEM((hidden, CELLS * 128), BF16),
            pltpu.VMEM((hidden, CELLS * 128), BF16),
        ],
        compiler_params=pltpu.CompilerParams(vmem_limit_bytes=24 * MIB),
        cost_estimate=pl.CostEstimate(
            flops=rows * 128 * 128 * hidden * 12,
            bytes_accessed=rows * 128 * 128 * 8,
            transcendentals=rows * 128 * hidden,
        ),
        name="column_network",
    )(in_hbm(cols), w_in_t, w_out_t, w_in, w_out, grads)


def totals_kernel(core, mine, other, in_total, out_total):
    scale = 1.0 / math.sqrt(SAMPLES)
    first = core[0] == 0
    for k in range(0, mine.shape[0], 128):
        at = slice(k, k + 128)
        here = mine[at, :].T
        there = other[at, :].T
        in_total[:, at] = jnp.where(first, here, there) * scale
        out_total[:, at] = jnp.where(first, there, here) * scale


def totals(core, mine, other):
    spec = pl.BlockSpec(memory_space=pltpu.VMEM)
    return pl.pallas_call(
        totals_kernel,
        in_specs=[pl.BlockSpec(memory_space=pltpu.SMEM), spec, spec],
        out_specs=[spec] * 2,
        out_shape=[jax.ShapeDtypeStruct(mine.shape[::-1], F32)] * 2,
        name="weight_totals",
    )(core, mine, other)


def last_kernel(
    start, blocks, first, first_next, back, back_next, speeds, inner, inner_next, outer,
    outer_next, west, low, high, *rest,
):
    out, grad, q_s, g_s, flux_s, drift_s = rest[-6:]
    here = lax.rem(pl.program_id(0) + start, blocks)
    quarter = blocks // 4

    def within(block):
        return jnp.logical_and(block >= quarter, block < blocks - quarter)

    def fill(fields):
        for i in range(LAST_ROWS):
            at = pl.ds(i * 16, 16)
            q_s[at, :] = first[i] + fields[i, 0].astype(F32)
            g_s[at, :] = back[i] + fields[i, 1].astype(F32)

    pl.when(within(here))(lambda: fill(inner))
    pl.when(jnp.logical_not(within(here)))(lambda: fill(outer))
    last = here == blocks - 1
    add = jnp.where(within(here + 1), inner_next[0].astype(F32), outer_next[0].astype(F32))
    q_s[LAST_ROWS * 16 :, :] = jnp.where(last, high[0], first_next[0] + add[0])
    g_s[LAST_ROWS * 16 :, :] = jnp.where(last, high[1], back_next[0] + add[1])
    q = row(q_s, 0)
    g = row(g_s, 0)
    edge = jnp.where(here == 0, low[...], west[...])
    flux, drift = west_terms(edge[0], q, edge[1], g, edge[2])
    fresh = jnp.logical_or(here == 0, pl.program_id(0) == 0)
    flux = jnp.where(fresh, flux, flux_s[...])
    drift = jnp.where(fresh, drift, drift_s[...])
    out2 = out.reshape(16 * LAST_ROWS, 128)
    grad2 = grad.reshape(16 * LAST_ROWS, 128)

    def one(i, carry):
        q, g, flux, drift = carry
        q_next = row(q_s, i + 1)
        g_next = row(g_s, i + 1)
        e = speeds[i, 0].astype(F32)
        n = speeds[i, 1].astype(F32)
        moved, pulled, flux, drift = step_row(q, q_next, g, g_next, e, n, flux, drift)
        put_rows(out2, i, LAST_ROWS, moved)
        put_rows(grad2, i, LAST_ROWS, pulled)
        return q_next, g_next, flux, drift

    carry = lax.fori_loop(0, LAST_ROWS, one, (q, g, flux, drift), unroll=UNROLL)
    flux_s[...] = carry[2]
    drift_s[...] = carry[3]


def last_step(start, count, first, back, speeds, inner, outer, west, low, high, shape, filled):
    width = shape[1]
    blocks = width // LAST_ROWS
    part = blocks // 4
    quarter = width // 4
    here = lambda s: lax.rem(s + start, blocks)

    def held(s):
        return jnp.clip(here(s) - part, 0, 2 * part - 1), 0, 0, 0

    def kept(s):
        b = here(s)
        return jnp.where(b < 3 * part, jnp.minimum(b + part, 2 * part - 1), b - 3 * part), 0, 0, 0

    after = lambda s: jnp.minimum((here(s) + 1) * LAST_ROWS, width - 1)

    def held_next(s):
        return jnp.clip(after(s) - quarter, 0, 2 * quarter - 1), 0, 0, 0

    def kept_next(s):
        r = after(s)
        far = jnp.clip(r - 3 * quarter, 0, 2 * quarter - 1)
        return jnp.where(r < quarter, r + quarter, far), 0, 0, 0

    field = pl.BlockSpec((LAST_ROWS, 16, 128), lambda s: (here(s), 0, 0))
    field_next = pl.BlockSpec((1, 16, 128), lambda s: (after(s), 0, 0))
    pair = lambda index: pl.BlockSpec((LAST_ROWS, 2, 16, 128), index)
    pair_next = lambda index: pl.BlockSpec((1, 2, 16, 128), index)
    whole = lambda n: pl.BlockSpec((n, 16, 128), lambda s: (0, 0, 0))
    result = pl.BlockSpec((16, LAST_ROWS, 128), lambda s: (0, here(s), 0))
    cells = count * LAST_ROWS * shape[0] * shape[2]
    return pl.pallas_call(
        functools.partial(last_kernel, start, blocks),
        grid=(count,),
        in_specs=[
            field, field_next, field, field_next, pair(lambda s: (here(s), 0, 0, 0)),
            pair(held), pair_next(held_next), pair(kept), pair_next(kept_next),
            whole(3), whole(3), whole(2),
        ]
        + [pl.BlockSpec(memory_space=pl.ANY)] * len(filled),
        out_specs=[result] * 2,
        out_shape=[pltpu.HBM(shape, F32)] * 2,
        input_output_aliases={12 + k: k for k in range(len(filled))},
        scratch_shapes=[pltpu.VMEM(((LAST_ROWS + 1) * 16, 128), F32)] * 2
        + [pltpu.VMEM((16, 128), F32)] * 2,
        compiler_params=pltpu.CompilerParams(vmem_limit_bytes=16 * MIB),
        cost_estimate=pl.CostEstimate(
            flops=cells * 40, bytes_accessed=cells * 24, transcendentals=0
        ),
        name="transport_two",
    )(
        *[in_hbm(x) for x in (first, first, back, back, speeds, inner, inner, outer, outer)],
        west, low, high, *filled,
    )


def shift(block, distance):
    count = lax.axis_size("tile")
    return lax.ppermute(block, "tile", [(i, (i + distance) % count) for i in range(count)])


def exchange(block):
    return lax.all_to_all(block, "lev", split_axis=0, concat_axis=0, tiled=True)


def partner(block, mask):
    return lax.ppermute(block, "tile", [(i, i ^ mask) for i in range(lax.axis_size("tile"))])


def chip_sum(grads):
    core = lax.rem(lax.axis_index("tile"), 2)
    mine = lax.dynamic_index_in_dim(grads, core, 0, False)
    other = lax.dynamic_index_in_dim(grads, 1 - core, 0, False)
    return mine + partner(other, 1)


def exchange_rows(block):
    lev = lax.axis_size("lev")
    groups = [
        [(y * 8 + rest) * lev + k for y in range(4) for k in range(lev)] for rest in range(8)
    ]
    return lax.all_to_all(
        block, ("tile", "lev"), split_axis=0, concat_axis=0, tiled=True, axis_index_groups=groups
    )


def z_sum(part):
    one, two, three = (partner(part, 2 * k) for k in (1, 2, 3))
    return (part + one) + (two + three)


def shards(state_in, east_speed, north_speed, w_in, w_out, cotangent):
    width = state_in.shape[1]
    blocks = width // ROWS
    hidden = w_in.shape[1]
    barrier = lax.optimization_barrier
    low, high = edge_rows(state_in, east_speed, cotangent)
    low, high, state_in = barrier((low, high, state_in))
    low = shift(low, 1)
    high = shift(high, -1)
    w_in_t, w_out_t = w_in.T, w_out.T
    none = jnp.zeros((3, 16, 128), F32)
    half = blocks // 2
    fields_in = (state_in, east_speed, north_speed, cotangent)
    first, back, speeds, cols_a = first_step(3 * blocks // 4, half, *fields_in, low, high, ())
    got_a = exchange(cols_a.reshape(8, width // 16, 2, 16, 128))
    held = (first, back, speeds)
    first, back, speeds, cols_b = first_step(
        blocks // 4, half, *fields_in, none, none[:2], held
    )
    got_b = exchange(cols_b.reshape(8, width // 16, 2, 16, 128))
    zero = jnp.zeros((2, hidden, 128), F32)
    outer, grads = network(got_a, w_in_t, w_out_t, w_in, w_out, zero)
    outer = exchange(outer)
    inner, grads = network(got_b, w_in_t, w_out_t, w_in, w_out, grads)
    part, outer = barrier((chip_sum(grads), outer))
    outer = outer.reshape(width // 2, 2, 16, 128)
    quarter = width // 4

    def edge(row):
        fields = outer[(row + quarter) % width]
        return jnp.stack([first[row], back[row]]) + fields.astype(F32)

    def west(row):
        return jnp.concatenate([edge(row), speeds[row, 0][None].astype(F32)])

    part, tail, head = barrier((part, edge(width - 1), edge(0)))
    part = jnp.sum(exchange_rows(part.reshape(32, hidden // 32, 128)), 0)
    low_next = jnp.concatenate([shift(tail, 1), low[2:]])
    high_next = shift(head, -1)
    part, inner, low_next, high_next = barrier((part, inner, low_next, high_next))
    inner = exchange(inner).reshape(width // 2, 2, 16, 128)
    fields_held = (first, back, speeds)
    shape = state_in.shape
    ends = shape[1] // LAST_ROWS
    results = last_step(
        ends - 1, 2, *fields_held, outer, outer, west(width - 1 - LAST_ROWS), low_next,
        high_next, shape, (),
    )
    part = z_sum(part)
    part, inner, *results = barrier((part, inner, *results))
    part = exchange_rows(jnp.broadcast_to(part[None], (32,) + part.shape)).reshape(hidden, 128)
    state_out, state_grad = last_step(
        1, ends - 2, *fields_held, inner, outer, west(LAST_ROWS - 1), low_next, high_next,
        shape, results,
    )
    part, state_out, state_grad = barrier((part, state_out, state_grad))
    core = lax.rem(lax.axis_index("tile"), 2)
    in_total, out_total = totals(core.reshape(1), part, partner(part, 1))
    return state_out, state_grad, in_total, out_total


def solution(mesh):
    field = P("lev", "tile", None)
    return jax.shard_map(
        shards,
        mesh=mesh,
        in_specs=(field, field, field, P(), P(), field),
        out_specs=(field, field, P(), P()),
        check_vma=False,
    )
```

```python
import functools
import math

import jax
import jax.numpy as jnp
from jax import lax
from jax.experimental import pallas as pl
from jax.experimental.pallas import tpu as pltpu
from jax.sharding import PartitionSpec as P

KAPPA = 0.05
SLOPE_C = 0.7978845608028654
CUBIC = 0.044715
ROWS = 64
LAST_ROWS = 32
SUB = 256
UNROLL = 16
SAMPLES = 8192 * 128
F32 = jnp.float32
BF16 = jnp.bfloat16
MIB = 1024 * 1024


def spread(pairs, tile):
    for ref, scratch in pairs:
        size = min(16, ref.shape[1])
        place = pl.multiple_of(tile * 16, size)
        part = ref[:, pl.ds(place, size), :].astype(F32)
        part = jnp.swapaxes(part, 0, 1).reshape(size * 16, 128)
        scratch[pl.ds(pl.multiple_of(tile * 256, 256), size * 16), :] = part


def row(ref, index):
    return ref[pl.ds(pl.multiple_of(index * 16, 16), 16), :]


def put_rows(ref, index, stride, value):
    ref[pl.ds(index, 8, stride), :] = value[:8]
    ref[pl.ds(index + 8 * stride, 8, stride), :] = value[8:]


def up_of(value):
    return pltpu.roll(value, value.shape[1] - 1, 1)


def down_of(value):
    return pltpu.roll(value, 1, 1)


def wall_mask(north):
    lane = lax.broadcasted_iota(jnp.int32, north.shape, 1)
    return jnp.where(lane < north.shape[1] - 1, north, 0.0)


def step_row(q, q_next, g, g_next, east, north, flux, drift):
    north = wall_mask(north)
    pos_east = jnp.maximum(east, 0.0) + KAPPA
    neg_east = jnp.minimum(east, 0.0) - KAPPA
    pos_north = jnp.maximum(north, 0.0)
    neg_north = jnp.minimum(north, 0.0)
    new_flux = pos_east * q + neg_east * q_next
    cross = pos_north * q + neg_north * up_of(q)
    moved = q - (new_flux - flux) - (cross - down_of(cross))
    ahead = g_next - g
    new_drift = neg_east * ahead
    above = up_of(g) - g
    pulled = (
        g + (pos_east * ahead + drift) + (pos_north * above + down_of(neg_north * above))
    )
    return moved, pulled, new_flux, new_drift


def west_terms(q_prev, q, g_prev, g, east_prev):
    pos = jnp.maximum(east_prev, 0.0) + KAPPA
    neg = jnp.minimum(east_prev, 0.0) - KAPPA
    return pos * q_prev + neg * q, neg * (g - g_prev)


def first_kernel(
    start, blocks, state, state_prev, state_next, cot, cot_prev, cot_next, east, east_prev,
    north, low, high, *rest,
):
    first, back, speeds, cols, q_s, g_s, east_s, north_s = rest[-13:-5]
    prev_s, gprev_s, next_s, gnext_s, eprev_s = rest[-5:]
    here = lax.rem(pl.program_id(0) + start, blocks)
    at_low = here == 0
    at_high = here == blocks - 1
    pairs = ((state, q_s), (cot, g_s), (east, east_s), (north, north_s))

    def spread_tile(tile, carry):
        spread(pairs, tile)
        return carry

    lax.fori_loop(0, ROWS // 16, spread_tile, 0)
    spread(((state_prev, prev_s), (cot_prev, gprev_s), (east_prev, eprev_s)), 0)
    spread(((state_next, next_s), (cot_next, gnext_s)), 0)
    q_prev = jnp.where(at_low, low[0], row(prev_s, 7))
    g_prev = jnp.where(at_low, low[1], row(gprev_s, 7))
    e_prev = jnp.where(at_low, low[2], row(eprev_s, 15))
    q_s[ROWS * 16 :, :] = jnp.where(at_high, high[0], row(next_s, 0))
    g_s[ROWS * 16 :, :] = jnp.where(at_high, high[1], row(gnext_s, 0))
    q = row(q_s, 0)
    g = row(g_s, 0)
    flux, drift = west_terms(q_prev, q, g_prev, g, e_prev)

    def one(i, carry):
        q, g, flux, drift = carry
        q_next = row(q_s, i + 1)
        g_next = row(g_s, i + 1)
        e = row(east_s, i)
        n = row(north_s, i)
        moved, pulled, flux, drift = step_row(q, q_next, g, g_next, e, n, flux, drift)
        first[i] = moved
        back[i] = pulled
        cols[i, 0] = moved.astype(BF16)
        cols[i, 1] = pulled.astype(BF16)
        speeds[i, 0] = e.astype(BF16)
        speeds[i, 1] = n.astype(BF16)
        return q_next, g_next, flux, drift

    lax.fori_loop(0, ROWS, one, (q, g, flux, drift), unroll=UNROLL)


def in_hbm(array):
    return pltpu.with_memory_space_constraint(array, pltpu.HBM)


def first_step(start, count, state, east, north, cot, low, high, filled):
    width = state.shape[1]
    blocks = width // ROWS
    here = lambda s: lax.rem(s + start, blocks)
    before = lambda s, size: lax.rem(here(s) * (ROWS // size) - 1 + width // size, width // size)
    after = lambda s, size: lax.rem((here(s) + 1) * (ROWS // size), width // size)
    main = pl.BlockSpec((16, ROWS, 128), lambda s: (0, here(s), 0))
    prev = pl.BlockSpec((16, 8, 128), lambda s: (0, before(s, 8), 0))
    prev16 = pl.BlockSpec((16, 16, 128), lambda s: (0, before(s, 16), 0))
    post = pl.BlockSpec((16, 8, 128), lambda s: (0, after(s, 8), 0))
    whole = lambda n: pl.BlockSpec((n, 16, 128), lambda s: (0, 0, 0))
    rows = count * ROWS
    field = pl.BlockSpec((ROWS, 16, 128), lambda s: (here(s), 0, 0))
    speed = pl.BlockSpec((ROWS, 2, 16, 128), lambda s: (here(s), 0, 0, 0))
    pair = pl.BlockSpec((ROWS, 2, 16, 128), lambda s: (s, 0, 0, 0))
    return pl.pallas_call(
        functools.partial(first_kernel, start, blocks),
        grid=(count,),
        in_specs=[main, prev, post, main, prev, post, main, prev16, main, whole(3), whole(2)]
        + [pl.BlockSpec(memory_space=pl.ANY)] * len(filled),
        out_specs=[field, field, speed, pair],
        out_shape=[
            pltpu.HBM((width, 16, 128), F32),
            pltpu.HBM((width, 16, 128), F32),
            pltpu.HBM((width, 2, 16, 128), BF16),
            pltpu.HBM((rows, 2, 16, 128), BF16),
        ],
        input_output_aliases={11 + k: k for k in range(len(filled))},
        scratch_shapes=[
            pltpu.VMEM(((ROWS + 1) * 16, 128), F32),
            pltpu.VMEM(((ROWS + 1) * 16, 128), F32),
            pltpu.VMEM((ROWS * 16, 128), F32),
            pltpu.VMEM((ROWS * 16, 128), F32),
            pltpu.VMEM((128, 128), F32),
            pltpu.VMEM((128, 128), F32),
            pltpu.VMEM((128, 128), F32),
            pltpu.VMEM((128, 128), F32),
            pltpu.VMEM((256, 128), F32),
        ],
        compiler_params=pltpu.CompilerParams(vmem_limit_bytes=16 * MIB),
        cost_estimate=pl.CostEstimate(
            flops=rows * 16 * 128 * 40, bytes_accessed=rows * 16 * 128 * 28, transcendentals=0
        ),
        name="transport_one",
    )(
        *[in_hbm(x) for x in (state, state, state, cot, cot, cot, east, east, north)],
        low,
        high,
        *filled,
    )


def edge_kernel(state_lo, state_hi, cot_lo, cot_hi, east_hi, low, high):
    low[0] = state_hi[:, 7, :]
    low[1] = cot_hi[:, 7, :]
    low[2] = east_hi[...].astype(F32)[:, 15, :]
    high[0] = state_lo[:, 0, :]
    high[1] = cot_lo[:, 0, :]


def edge_rows(state, east, cot):
    width = state.shape[1]
    head = pl.BlockSpec((16, 8, 128), lambda s: (0, 0, 0))
    tail = pl.BlockSpec((16, 8, 128), lambda s: (0, width // 8 - 1, 0))
    tail16 = pl.BlockSpec((16, 16, 128), lambda s: (0, width // 16 - 1, 0))
    return pl.pallas_call(
        edge_kernel,
        grid=(1,),
        in_specs=[head, tail, head, tail, tail16],
        out_specs=[
            pl.BlockSpec((3, 16, 128), lambda s: (0, 0, 0)),
            pl.BlockSpec((2, 16, 128), lambda s: (0, 0, 0)),
        ],
        out_shape=[
            jax.ShapeDtypeStruct((3, 16, 128), F32),
            jax.ShapeDtypeStruct((2, 16, 128), F32),
        ],
        name="edge_rows",
    )(*[in_hbm(x) for x in (state, state, cot, cot, east)])


CELLS = 8
HTILE = 256


def network_kernel(cols, w_in_t, w_out_t, w_in, w_out, fields, grads, act_s, dpre_s):
    hidden = w_in_t.shape[0]

    @pl.when(pl.program_id(0) == 0)
    def _():
        grads[...] = jnp.zeros_like(grads)

    col = jnp.concatenate([cols[:, i, 0].reshape(128, 128) for i in range(CELLS)], 1)
    gcol = jnp.concatenate([cols[:, i, 1].reshape(128, 128) for i in range(CELLS)], 1)
    for h in range(0, hidden, HTILE):
        part = slice(h, h + HTILE)
        for n in range(0, CELLS * 128, SUB):
            at = slice(n, n + SUB)
            z = jnp.dot(w_in_t[part, :], col[:, at], preferred_element_type=F32)
            d_act = jnp.dot(w_out_t[part, :], gcol[:, at], preferred_element_type=F32)
            z2 = z * z
            t = jnp.tanh(z * (z2 * (SLOPE_C * CUBIC) + SLOPE_C))
            part_t = 0.5 * t
            half = part_t + 0.5
            act = z * half
            slope = half + act * (0.5 - part_t) * (
                z2 * (6.0 * SLOPE_C * CUBIC) + 2.0 * SLOPE_C
            )
            act_s[part, at] = act.astype(BF16)
            dpre_s[part, at] = (d_act * slope).astype(BF16)
    nt = (((1,), (1,)), ((), ()))
    grads[0] += lax.dot_general(dpre_s[...], col, nt, preferred_element_type=F32)
    grads[1] += lax.dot_general(act_s[...], gcol, nt, preferred_element_type=F32)
    tend = jnp.dot(w_out[...], act_s[...], preferred_element_type=F32).astype(BF16)
    d_cols = jnp.dot(w_in[...], dpre_s[...], preferred_element_type=F32).astype(BF16)
    for i in range(CELLS):
        fields[:, i, 0] = tend[:, i * 128 : (i + 1) * 128].reshape(8, 16, 128)
        fields[:, i, 1] = d_cols[:, i * 128 : (i + 1) * 128].reshape(8, 16, 128)


def network(cols, w_in_t, w_out_t, w_in, w_out):
    rows = cols.shape[1]
    hidden = w_in.shape[1]
    block = pl.BlockSpec((8, CELLS, 2, 16, 128), lambda s: (0, s, 0, 0, 0))
    tall = pl.BlockSpec((hidden, 128), lambda s: (0, 0))
    wide = pl.BlockSpec((128, hidden), lambda s: (0, 0))
    total = pl.BlockSpec((2, hidden, 128), lambda s: (0, 0, 0))
    return pl.pallas_call(
        functools.partial(network_kernel),
        grid=(rows // CELLS,),
        in_specs=[block, tall, tall, wide, wide],
        out_specs=[block, total],
        out_shape=[
            pltpu.HBM(cols.shape, BF16),
            jax.ShapeDtypeStruct((2, hidden, 128), F32),
        ],
        scratch_shapes=[
            pltpu.VMEM((hidden, CELLS * 128), BF16),
            pltpu.VMEM((hidden, CELLS * 128), BF16),
        ],
        compiler_params=pltpu.CompilerParams(vmem_limit_bytes=24 * MIB),
        cost_estimate=pl.CostEstimate(
            flops=rows * 128 * 128 * hidden * 12,
            bytes_accessed=rows * 128 * 128 * 8,
            transcendentals=rows * 128 * hidden,
        ),
        name="column_network",
    )(cols, *[in_hbm(x) for x in (w_in_t, w_out_t, w_in, w_out)])


def totals_kernel(core, sums, in_total, out_total):
    scale = 1.0 / math.sqrt(SAMPLES)
    first = core[0] == 0
    size = sums.shape[2]
    for k in range(0, sums.shape[0], 128 // size):
        pick = range(k, k + 128 // size)
        at = slice(k * size, k * size + 128)
        here = jnp.concatenate([sums[i, 0] for i in pick], 0).astype(F32).T
        there = jnp.concatenate([sums[i, 1] for i in pick], 0).astype(F32).T
        in_total[:, at] = jnp.where(first, here, there) * scale
        out_total[:, at] = jnp.where(first, there, here) * scale


def totals(core, sums):
    count, _, size, rows = sums.shape
    out = pl.BlockSpec((rows, count * size), lambda s: (0, 0))
    return pl.pallas_call(
        totals_kernel,
        grid=(1,),
        in_specs=[
            pl.BlockSpec(memory_space=pltpu.SMEM),
            pl.BlockSpec(sums.shape, lambda s: (0, 0, 0, 0)),
        ],
        out_specs=[out] * 2,
        out_shape=[pltpu.HBM((rows, count * size), F32)] * 2,
        compiler_params=pltpu.CompilerParams(vmem_limit_bytes=8 * MIB),
        name="weight_totals",
    )(core, sums)


def last_kernel(
    start, blocks, first, first_next, back, back_next, speeds, inner, inner_next, outer,
    outer_next, west, low, high, *rest,
):
    out, grad, q_s, g_s, flux_s, drift_s = rest[-6:]
    here = lax.rem(pl.program_id(0) + start, blocks)
    quarter = blocks // 4

    def within(block):
        return jnp.logical_and(block >= quarter, block < blocks - quarter)

    def fill(fields):
        for i in range(LAST_ROWS):
            at = pl.ds(i * 16, 16)
            q_s[at, :] = first[i] + fields[i, 0].astype(F32)
            g_s[at, :] = back[i] + fields[i, 1].astype(F32)

    pl.when(within(here))(lambda: fill(inner))
    pl.when(jnp.logical_not(within(here)))(lambda: fill(outer))
    last = here == blocks - 1
    add = jnp.where(within(here + 1), inner_next[0].astype(F32), outer_next[0].astype(F32))
    q_s[LAST_ROWS * 16 :, :] = jnp.where(last, high[0], first_next[0] + add[0])
    g_s[LAST_ROWS * 16 :, :] = jnp.where(last, high[1], back_next[0] + add[1])
    q = row(q_s, 0)
    g = row(g_s, 0)
    edge = jnp.where(here == 0, low[...], west[...])
    flux, drift = west_terms(edge[0], q, edge[1], g, edge[2])
    fresh = jnp.logical_or(here == 0, pl.program_id(0) == 0)
    flux = jnp.where(fresh, flux, flux_s[...])
    drift = jnp.where(fresh, drift, drift_s[...])
    out2 = out.reshape(16 * LAST_ROWS, 128)
    grad2 = grad.reshape(16 * LAST_ROWS, 128)

    def one(i, carry):
        q, g, flux, drift = carry
        q_next = row(q_s, i + 1)
        g_next = row(g_s, i + 1)
        e = speeds[i, 0].astype(F32)
        n = speeds[i, 1].astype(F32)
        moved, pulled, flux, drift = step_row(q, q_next, g, g_next, e, n, flux, drift)
        put_rows(out2, i, LAST_ROWS, moved)
        put_rows(grad2, i, LAST_ROWS, pulled)
        return q_next, g_next, flux, drift

    carry = lax.fori_loop(0, LAST_ROWS, one, (q, g, flux, drift), unroll=UNROLL)
    flux_s[...] = carry[2]
    drift_s[...] = carry[3]


def last_step(start, count, first, back, speeds, inner, outer, west, low, high, shape, filled):
    width = shape[1]
    blocks = width // LAST_ROWS
    part = blocks // 4
    quarter = width // 4
    here = lambda s: lax.rem(s + start, blocks)

    def held(s):
        return jnp.clip(here(s) - part, 0, 2 * part - 1), 0, 0, 0

    def kept(s):
        b = here(s)
        return jnp.where(b < 3 * part, jnp.minimum(b + part, 2 * part - 1), b - 3 * part), 0, 0, 0

    after = lambda s: jnp.minimum((here(s) + 1) * LAST_ROWS, width - 1)

    def held_next(s):
        return jnp.clip(after(s) - quarter, 0, 2 * quarter - 1), 0, 0, 0

    def kept_next(s):
        r = after(s)
        far = jnp.clip(r - 3 * quarter, 0, 2 * quarter - 1)
        return jnp.where(r < quarter, r + quarter, far), 0, 0, 0

    field = pl.BlockSpec((LAST_ROWS, 16, 128), lambda s: (here(s), 0, 0))
    field_next = pl.BlockSpec((1, 16, 128), lambda s: (after(s), 0, 0))
    pair = lambda index: pl.BlockSpec((LAST_ROWS, 2, 16, 128), index)
    pair_next = lambda index: pl.BlockSpec((1, 2, 16, 128), index)
    whole = lambda n: pl.BlockSpec((n, 16, 128), lambda s: (0, 0, 0))
    result = pl.BlockSpec((16, LAST_ROWS, 128), lambda s: (0, here(s), 0))
    cells = count * LAST_ROWS * shape[0] * shape[2]
    return pl.pallas_call(
        functools.partial(last_kernel, start, blocks),
        grid=(count,),
        in_specs=[
            field, field_next, field, field_next, pair(lambda s: (here(s), 0, 0, 0)),
            pair(held), pair_next(held_next), pair(kept), pair_next(kept_next),
            whole(3), whole(3), whole(2),
        ]
        + [pl.BlockSpec(memory_space=pl.ANY)] * len(filled),
        out_specs=[result] * 2,
        out_shape=[pltpu.HBM(shape, F32)] * 2,
        input_output_aliases={12 + k: k for k in range(len(filled))},
        scratch_shapes=[pltpu.VMEM(((LAST_ROWS + 1) * 16, 128), F32)] * 2
        + [pltpu.VMEM((16, 128), F32)] * 2,
        compiler_params=pltpu.CompilerParams(vmem_limit_bytes=16 * MIB),
        cost_estimate=pl.CostEstimate(
            flops=cells * 40, bytes_accessed=cells * 24, transcendentals=0
        ),
        name="transport_two",
    )(
        *[in_hbm(x) for x in (first, first, back, back, speeds)],
        inner, inner, outer, outer, west, low, high, *filled,
    )


def shift(block, distance):
    count = lax.axis_size("tile")
    return lax.ppermute(block, "tile", [(i, (i + distance) % count) for i in range(count)])


def exchange(block):
    return lax.all_to_all(block, "lev", split_axis=0, concat_axis=0, tiled=True)


def partner(block, mask):
    return lax.ppermute(block, "tile", [(i, i ^ mask) for i in range(lax.axis_size("tile"))])


def chip_sum(grads):
    core = lax.rem(lax.axis_index("tile"), 2)
    mine = lax.dynamic_index_in_dim(grads, core, 0, False)
    other = lax.dynamic_index_in_dim(grads, 1 - core, 0, False)
    return mine + partner(other, 1)


def exchange_rows(block):
    lev = lax.axis_size("lev")
    groups = [
        [(y * 8 + rest) * lev + k for y in range(4) for k in range(lev)] for rest in range(8)
    ]
    return lax.all_to_all(
        block, ("tile", "lev"), split_axis=0, concat_axis=0, tiled=True, axis_index_groups=groups
    )


def z_sum(part):
    one, two, three = (partner(part, 2 * k) for k in (1, 2, 3))
    return (part + one) + (two + three)


def shards(state_in, east_speed, north_speed, w_in, w_out, cotangent):
    width = state_in.shape[1]
    blocks = width // ROWS
    hidden = w_in.shape[1]
    barrier = lax.optimization_barrier
    low, high = edge_rows(state_in, east_speed, cotangent)
    low, high, state_in = barrier((low, high, state_in))
    low = shift(low, 1)
    high = shift(high, -1)
    w_in_t, w_out_t = w_in.T, w_out.T
    none = jnp.zeros((3, 16, 128), F32)
    half = blocks // 2
    fields_in = (state_in, east_speed, north_speed, cotangent)
    first, back, speeds, cols_a = first_step(3 * blocks // 4, half, *fields_in, low, high, ())
    got_a = exchange(cols_a.reshape(8, width // 16, 2, 16, 128))
    held = (first, back, speeds)
    first, back, speeds, cols_b = first_step(
        blocks // 4, half, *fields_in, none, none[:2], held
    )
    got_b = exchange(cols_b.reshape(8, width // 16, 2, 16, 128))
    outer, grads_a = network(got_a, w_in_t, w_out_t, w_in, w_out)
    outer = exchange(outer)
    inner, grads_b = network(got_b, w_in_t, w_out_t, w_in, w_out)
    part, outer = barrier((chip_sum(grads_a + grads_b), outer))
    outer = outer.reshape(width // 2, 2, 16, 128)
    quarter = width // 4

    def edge(row):
        fields = outer[(row + quarter) % width]
        return jnp.stack([first[row], back[row]]) + fields.astype(F32)

    def west(row):
        return jnp.concatenate([edge(row), speeds[row, 0][None].astype(F32)])

    part = jnp.sum(exchange_rows(part.reshape(32, hidden // 32, 128)), 0)
    low_next = jnp.concatenate([shift(edge(width - 1), 1), low[2:]])
    high_next = shift(edge(0), -1)
    part, inner, low_next, high_next = barrier((part, inner, low_next, high_next))
    inner = exchange(inner).reshape(width // 2, 2, 16, 128)
    fields_held = (first, back, speeds)
    shape = state_in.shape
    ends = shape[1] // LAST_ROWS
    results = last_step(
        ends - 1, 2, *fields_held, outer, outer, west(width - 1 - LAST_ROWS), low_next,
        high_next, shape, (),
    )
    part = z_sum(jnp.stack([part, partner(part, 1)])).astype(BF16)
    part, inner, *results = barrier((part, inner, *results))
    part = exchange_rows(jnp.broadcast_to(part[None], (32,) + part.shape))
    state_out, state_grad = last_step(
        1, ends - 2, *fields_held, inner, outer, west(LAST_ROWS - 1), low_next, high_next,
        shape, results,
    )
    part, state_out, state_grad = barrier((part, state_out, state_grad))
    core = lax.rem(lax.axis_index("tile"), 2)
    in_total, out_total = totals(core.reshape(1), part)
    return state_out, state_grad, in_total, out_total


def solution(mesh):
    field = P("lev", "tile", None)
    return jax.shard_map(
        shards,
        mesh=mesh,
        in_specs=(field, field, field, P(), P(), field),
        out_specs=(field, field, P(), P()),
        check_vma=False,
    )
```

```python
import functools
import math

import jax
import jax.numpy as jnp
from jax import lax
from jax.experimental import pallas as pl
from jax.experimental.pallas import tpu as pltpu
from jax.sharding import PartitionSpec as P

KAPPA = 0.05
SLOPE_C = 0.7978845608028654
CUBIC = 0.044715
ROWS = 64
LAST_ROWS = 64
SUB = 256
UNROLL = 16
SAMPLES = 8192 * 128
F32 = jnp.float32
BF16 = jnp.bfloat16
MIB = 1024 * 1024


def spread(pairs, tile):
    for ref, scratch in pairs:
        size = min(16, ref.shape[1])
        place = pl.multiple_of(tile * 16, size)
        part = ref[:, pl.ds(place, size), :].astype(F32)
        part = jnp.swapaxes(part, 0, 1).reshape(size * 16, 128)
        scratch[pl.ds(pl.multiple_of(tile * 256, 256), size * 16), :] = part


def row(ref, index):
    return ref[pl.ds(pl.multiple_of(index * 16, 16), 16), :]


def gather(scratch, ref, rows):
    def one(tile, carry):
        part = scratch[pl.ds(pl.multiple_of(tile * 256, 256), 256), :].reshape(16, 16, 128)
        ref[:, pl.ds(pl.multiple_of(tile * 16, 16), 16), :] = jnp.swapaxes(part, 0, 1)
        return carry

    lax.fori_loop(0, rows // 16, one, 0)


def up_of(value):
    return pltpu.roll(value, value.shape[1] - 1, 1)


def down_of(value):
    return pltpu.roll(value, 1, 1)


def wall_mask(north):
    lane = lax.broadcasted_iota(jnp.int32, north.shape, 1)
    return jnp.where(lane < north.shape[1] - 1, north, 0.0)


def step_row(q, q_next, g, g_next, east, north, flux, drift):
    north = wall_mask(north)
    pos_east = jnp.maximum(east, 0.0) + KAPPA
    neg_east = jnp.minimum(east, 0.0) - KAPPA
    pos_north = jnp.maximum(north, 0.0)
    neg_north = jnp.minimum(north, 0.0)
    new_flux = pos_east * q + neg_east * q_next
    cross = pos_north * q + neg_north * up_of(q)
    moved = q - (new_flux - flux) - (cross - down_of(cross))
    ahead = g_next - g
    new_drift = neg_east * ahead
    above = up_of(g) - g
    pulled = (
        g + (pos_east * ahead + drift) + (pos_north * above + down_of(neg_north * above))
    )
    return moved, pulled, new_flux, new_drift


def west_terms(q_prev, q, g_prev, g, east_prev):
    pos = jnp.maximum(east_prev, 0.0) + KAPPA
    neg = jnp.minimum(east_prev, 0.0) - KAPPA
    return pos * q_prev + neg * q, neg * (g - g_prev)


def first_kernel(
    start, blocks, state, state_prev, state_next, cot, cot_prev, cot_next, east, east_prev,
    north, low, high, *rest,
):
    first, back, speeds, cols, q_s, g_s, east_s, north_s = rest[-13:-5]
    prev_s, gprev_s, next_s, gnext_s, eprev_s = rest[-5:]
    here = lax.rem(pl.program_id(0) + start, blocks)
    at_low = here == 0
    at_high = here == blocks - 1
    pairs = ((state, q_s), (cot, g_s), (east, east_s), (north, north_s))

    def spread_tile(tile, carry):
        spread(pairs, tile)
        return carry

    lax.fori_loop(0, ROWS // 16, spread_tile, 0)
    spread(((state_prev, prev_s), (cot_prev, gprev_s), (east_prev, eprev_s)), 0)
    spread(((state_next, next_s), (cot_next, gnext_s)), 0)
    q_prev = jnp.where(at_low, low[0], row(prev_s, 7))
    g_prev = jnp.where(at_low, low[1], row(gprev_s, 7))
    e_prev = jnp.where(at_low, low[2], row(eprev_s, 15))
    q_s[ROWS * 16 :, :] = jnp.where(at_high, high[0], row(next_s, 0))
    g_s[ROWS * 16 :, :] = jnp.where(at_high, high[1], row(gnext_s, 0))
    q = row(q_s, 0)
    g = row(g_s, 0)
    flux, drift = west_terms(q_prev, q, g_prev, g, e_prev)

    def one(i, carry):
        q, g, flux, drift = carry
        q_next = row(q_s, i + 1)
        g_next = row(g_s, i + 1)
        e = row(east_s, i)
        n = row(north_s, i)
        moved, pulled, flux, drift = step_row(q, q_next, g, g_next, e, n, flux, drift)
        first[i] = moved
        back[i] = pulled
        cols[i, 0] = moved.astype(BF16)
        cols[i, 1] = pulled.astype(BF16)
        speeds[i, 0] = e.astype(BF16)
        speeds[i, 1] = n.astype(BF16)
        return q_next, g_next, flux, drift

    lax.fori_loop(0, ROWS, one, (q, g, flux, drift), unroll=UNROLL)


def in_hbm(array):
    return pltpu.with_memory_space_constraint(array, pltpu.HBM)


def first_step(start, count, state, east, north, cot, low, high, filled):
    width = state.shape[1]
    blocks = width // ROWS
    here = lambda s: lax.rem(s + start, blocks)
    before = lambda s, size: lax.rem(here(s) * (ROWS // size) - 1 + width // size, width // size)
    after = lambda s, size: lax.rem((here(s) + 1) * (ROWS // size), width // size)
    main = pl.BlockSpec((16, ROWS, 128), lambda s: (0, here(s), 0))
    prev = pl.BlockSpec((16, 8, 128), lambda s: (0, before(s, 8), 0))
    prev16 = pl.BlockSpec((16, 16, 128), lambda s: (0, before(s, 16), 0))
    post = pl.BlockSpec((16, 8, 128), lambda s: (0, after(s, 8), 0))
    whole = lambda n: pl.BlockSpec((n, 16, 128), lambda s: (0, 0, 0))
    rows = count * ROWS
    field = pl.BlockSpec((ROWS, 16, 128), lambda s: (here(s), 0, 0))
    speed = pl.BlockSpec((ROWS, 2, 16, 128), lambda s: (here(s), 0, 0, 0))
    pair = pl.BlockSpec((ROWS, 2, 16, 128), lambda s: (s, 0, 0, 0))
    return pl.pallas_call(
        functools.partial(first_kernel, start, blocks),
        grid=(count,),
        in_specs=[main, prev, post, main, prev, post, main, prev16, main, whole(3), whole(3)]
        + [pl.BlockSpec(memory_space=pl.ANY)] * len(filled),
        out_specs=[field, field, speed, pair],
        out_shape=[
            pltpu.HBM((width, 16, 128), F32),
            pltpu.HBM((width, 16, 128), F32),
            pltpu.HBM((width, 2, 16, 128), BF16),
            pltpu.HBM((rows, 2, 16, 128), BF16),
        ],
        input_output_aliases={11 + k: k for k in range(len(filled))},
        scratch_shapes=[
            pltpu.VMEM(((ROWS + 1) * 16, 128), F32),
            pltpu.VMEM(((ROWS + 1) * 16, 128), F32),
            pltpu.VMEM((ROWS * 16, 128), F32),
            pltpu.VMEM((ROWS * 16, 128), F32),
            pltpu.VMEM((128, 128), F32),
            pltpu.VMEM((128, 128), F32),
            pltpu.VMEM((128, 128), F32),
            pltpu.VMEM((128, 128), F32),
            pltpu.VMEM((256, 128), F32),
        ],
        compiler_params=pltpu.CompilerParams(vmem_limit_bytes=16 * MIB),
        cost_estimate=pl.CostEstimate(
            flops=rows * 16 * 128 * 40, bytes_accessed=rows * 16 * 128 * 28, transcendentals=0
        ),
        name="transport_one",
    )(
        *[in_hbm(x) for x in (state, state, state, cot, cot, cot, east, east, north)],
        low,
        high,
        *filled,
    )


def edge_kernel(state_lo, state_hi, cot_lo, cot_hi, east_hi, low, high):
    low[0] = state_hi[:, 7, :]
    low[1] = cot_hi[:, 7, :]
    low[2] = east_hi[...].astype(F32)[:, 15, :]
    high[0] = state_lo[:, 0, :]
    high[1] = cot_lo[:, 0, :]
    high[2] = cot_lo[:, 0, :]


def edge_rows(state, east, cot):
    width = state.shape[1]
    head = pl.BlockSpec((16, 8, 128), lambda s: (0, 0, 0))
    tail = pl.BlockSpec((16, 8, 128), lambda s: (0, width // 8 - 1, 0))
    tail16 = pl.BlockSpec((16, 16, 128), lambda s: (0, width // 16 - 1, 0))
    return pl.pallas_call(
        edge_kernel,
        grid=(1,),
        in_specs=[head, tail, head, tail, tail16],
        out_specs=[
            pl.BlockSpec((3, 16, 128), lambda s: (0, 0, 0)),
            pl.BlockSpec((3, 16, 128), lambda s: (0, 0, 0)),
        ],
        out_shape=[
            jax.ShapeDtypeStruct((3, 16, 128), F32),
            jax.ShapeDtypeStruct((3, 16, 128), F32),
        ],
        name="edge_rows",
    )(*[in_hbm(x) for x in (state, state, cot, cot, east)])


CELLS = 8
HTILE = 256


def network_kernel(cols, w_in_t, w_out_t, w_in, w_out, fields, grads, act_s, dpre_s):
    hidden = w_in_t.shape[0]

    @pl.when(pl.program_id(0) == 0)
    def _():
        grads[...] = jnp.zeros_like(grads)

    col = jnp.concatenate([cols[:, i, 0].reshape(128, 128) for i in range(CELLS)], 1)
    gcol = jnp.concatenate([cols[:, i, 1].reshape(128, 128) for i in range(CELLS)], 1)
    for h in range(0, hidden, HTILE):
        part = slice(h, h + HTILE)
        for n in range(0, CELLS * 128, SUB):
            at = slice(n, n + SUB)
            z = jnp.dot(w_in_t[part, :], col[:, at], preferred_element_type=F32)
            d_act = jnp.dot(w_out_t[part, :], gcol[:, at], preferred_element_type=F32)
            z2 = z * z
            t = jnp.tanh(z * (z2 * (SLOPE_C * CUBIC) + SLOPE_C))
            part_t = 0.5 * t
            half = part_t + 0.5
            act = z * half
            slope = half + act * (0.5 - part_t) * (
                z2 * (6.0 * SLOPE_C * CUBIC) + 2.0 * SLOPE_C
            )
            act_s[part, at] = act.astype(BF16)
            dpre_s[part, at] = (d_act * slope).astype(BF16)
    nt = (((1,), (1,)), ((), ()))
    grads[0] += lax.dot_general(dpre_s[...], col, nt, preferred_element_type=F32)
    grads[1] += lax.dot_general(act_s[...], gcol, nt, preferred_element_type=F32)
    tend = jnp.dot(w_out[...], act_s[...], preferred_element_type=F32).astype(BF16)
    d_cols = jnp.dot(w_in[...], dpre_s[...], preferred_element_type=F32).astype(BF16)
    for i in range(CELLS):
        fields[:, i, 0] = tend[:, i * 128 : (i + 1) * 128].reshape(8, 16, 128)
        fields[:, i, 1] = d_cols[:, i * 128 : (i + 1) * 128].reshape(8, 16, 128)


def network(cols, w_in_t, w_out_t, w_in, w_out):
    rows = cols.shape[1]
    hidden = w_in.shape[1]
    block = pl.BlockSpec((8, CELLS, 2, 16, 128), lambda s: (0, s, 0, 0, 0))
    tall = pl.BlockSpec((hidden, 128), lambda s: (0, 0))
    wide = pl.BlockSpec((128, hidden), lambda s: (0, 0))
    total = pl.BlockSpec((2, hidden, 128), lambda s: (0, 0, 0))
    return pl.pallas_call(
        functools.partial(network_kernel),
        grid=(rows // CELLS,),
        in_specs=[block, tall, tall, wide, wide],
        out_specs=[block, total],
        out_shape=[
            pltpu.HBM(cols.shape, BF16),
            jax.ShapeDtypeStruct((2, hidden, 128), F32),
        ],
        scratch_shapes=[
            pltpu.VMEM((hidden, CELLS * 128), BF16),
            pltpu.VMEM((hidden, CELLS * 128), BF16),
        ],
        compiler_params=pltpu.CompilerParams(vmem_limit_bytes=24 * MIB),
        cost_estimate=pl.CostEstimate(
            flops=rows * 128 * 128 * hidden * 12,
            bytes_accessed=rows * 128 * 128 * 8,
            transcendentals=rows * 128 * hidden,
        ),
        name="column_network",
    )(cols, *[in_hbm(x) for x in (w_in_t, w_out_t, w_in, w_out)])


def totals_kernel(core, sums, in_total, out_total):
    scale = 1.0 / math.sqrt(SAMPLES)
    first = core[0] == 0
    size = sums.shape[2]
    for k in range(0, sums.shape[0], 128 // size):
        pick = range(k, k + 128 // size)
        at = slice(k * size, k * size + 128)
        here = jnp.concatenate([sums[i, 0] for i in pick], 0).astype(F32).T
        there = jnp.concatenate([sums[i, 1] for i in pick], 0).astype(F32).T
        in_total[:, at] = jnp.where(first, here, there) * scale
        out_total[:, at] = jnp.where(first, there, here) * scale


def totals(core, sums):
    count, _, size, rows = sums.shape
    out = pl.BlockSpec((rows, count * size), lambda s: (0, 0))
    return pl.pallas_call(
        totals_kernel,
        grid=(1,),
        in_specs=[
            pl.BlockSpec(memory_space=pltpu.SMEM),
            pl.BlockSpec(sums.shape, lambda s: (0, 0, 0, 0)),
        ],
        out_specs=[out] * 2,
        out_shape=[pltpu.HBM((rows, count * size), F32)] * 2,
        compiler_params=pltpu.CompilerParams(vmem_limit_bytes=8 * MIB),
        name="weight_totals",
    )(core, sums)


def last_kernel(
    start, blocks, first, first_next, back, back_next, speeds, inner, inner_next, outer,
    outer_next, west, low, high, *rest,
):
    out, grad, q_s, g_s, out_s, grad_s, flux_s, drift_s = rest[-8:]
    here = lax.rem(pl.program_id(0) + start, blocks)
    quarter = blocks // 4

    def within(block):
        return jnp.logical_and(block >= quarter, block < blocks - quarter)

    def fill(fields):
        for i in range(LAST_ROWS):
            at = pl.ds(i * 16, 16)
            q_s[at, :] = first[i] + fields[i, 0].astype(F32)
            g_s[at, :] = back[i] + fields[i, 1].astype(F32)

    pl.when(within(here))(lambda: fill(inner))
    pl.when(jnp.logical_not(within(here)))(lambda: fill(outer))
    last = here == blocks - 1
    add = jnp.where(within(here + 1), inner_next[0].astype(F32), outer_next[0].astype(F32))
    q_s[LAST_ROWS * 16 :, :] = jnp.where(last, high[0], first_next[0] + add[0])
    g_s[LAST_ROWS * 16 :, :] = jnp.where(last, high[1], back_next[0] + add[1])
    q = row(q_s, 0)
    g = row(g_s, 0)
    edge = jnp.where(here == 0, low[...], west[...])
    flux, drift = west_terms(edge[0], q, edge[1], g, edge[2])
    fresh = jnp.logical_or(here == 0, pl.program_id(0) == 0)
    flux = jnp.where(fresh, flux, flux_s[...])
    drift = jnp.where(fresh, drift, drift_s[...])
    def one(i, carry):
        q, g, flux, drift = carry
        q_next = row(q_s, i + 1)
        g_next = row(g_s, i + 1)
        e = speeds[i, 0].astype(F32)
        n = speeds[i, 1].astype(F32)
        moved, pulled, flux, drift = step_row(q, q_next, g, g_next, e, n, flux, drift)
        at = pl.ds(pl.multiple_of(i * 16, 16), 16)
        out_s[at, :] = moved
        grad_s[at, :] = pulled
        return q_next, g_next, flux, drift

    carry = lax.fori_loop(0, LAST_ROWS, one, (q, g, flux, drift), unroll=UNROLL)
    flux_s[...] = carry[2]
    drift_s[...] = carry[3]
    gather(out_s, out, LAST_ROWS)
    gather(grad_s, grad, LAST_ROWS)


def last_step(start, count, first, back, speeds, inner, outer, west, low, high, shape, filled):
    width = shape[1]
    blocks = width // LAST_ROWS
    part = blocks // 4
    quarter = width // 4
    here = lambda s: lax.rem(s + start, blocks)

    def held(s):
        return jnp.clip(here(s) - part, 0, 2 * part - 1), 0, 0, 0

    def kept(s):
        b = here(s)
        return jnp.where(b < 3 * part, jnp.minimum(b + part, 2 * part - 1), b - 3 * part), 0, 0, 0

    after = lambda s: jnp.minimum((here(s) + 1) * LAST_ROWS, width - 1)

    def held_next(s):
        return jnp.clip(after(s) - quarter, 0, 2 * quarter - 1), 0, 0, 0

    def kept_next(s):
        r = after(s)
        far = jnp.clip(r - 3 * quarter, 0, 2 * quarter - 1)
        return jnp.where(r < quarter, r + quarter, far), 0, 0, 0

    field = pl.BlockSpec((LAST_ROWS, 16, 128), lambda s: (here(s), 0, 0))
    field_next = pl.BlockSpec((1, 16, 128), lambda s: (after(s), 0, 0))
    pair = lambda index: pl.BlockSpec((LAST_ROWS, 2, 16, 128), index)
    pair_next = lambda index: pl.BlockSpec((1, 2, 16, 128), index)
    whole = lambda n: pl.BlockSpec((n, 16, 128), lambda s: (0, 0, 0))
    result = pl.BlockSpec((16, LAST_ROWS, 128), lambda s: (0, here(s), 0))
    cells = count * LAST_ROWS * shape[0] * shape[2]
    return pl.pallas_call(
        functools.partial(last_kernel, start, blocks),
        grid=(count,),
        in_specs=[
            field, field_next, field, field_next, pair(lambda s: (here(s), 0, 0, 0)),
            pair(held), pair_next(held_next), pair(kept), pair_next(kept_next),
            whole(3), whole(3), whole(2),
        ]
        + [pl.BlockSpec(memory_space=pl.ANY)] * len(filled),
        out_specs=[result] * 2,
        out_shape=[pltpu.HBM(shape, F32)] * 2,
        input_output_aliases={12 + k: k for k in range(len(filled))},
        scratch_shapes=[pltpu.VMEM(((LAST_ROWS + 1) * 16, 128), F32)] * 2
        + [pltpu.VMEM((LAST_ROWS * 16, 128), F32)] * 2
        + [pltpu.VMEM((16, 128), F32)] * 2,
        compiler_params=pltpu.CompilerParams(vmem_limit_bytes=16 * MIB),
        cost_estimate=pl.CostEstimate(
            flops=cells * 40, bytes_accessed=cells * 24, transcendentals=0
        ),
        name="transport_two",
    )(
        *[in_hbm(x) for x in (first, first, back, back, speeds)],
        inner, inner, outer, outer, west, low, high, *filled,
    )


def across(block):
    count = lax.axis_size("tile")
    return lax.ppermute(
        block, "tile", [(i, (i + 1 if i % 2 else i - 1) % count) for i in range(count)]
    )


def halo(core, last, first):
    even = core == 0
    by_link = across(jnp.where(even, first, last))
    by_chip = partner(jnp.where(even, last, first), 1)
    return jnp.where(even, by_link, by_chip), jnp.where(even, by_chip, by_link)


def exchange(block):
    return lax.all_to_all(block, "lev", split_axis=0, concat_axis=0, tiled=True)


def partner(block, mask):
    return lax.ppermute(block, "tile", [(i, i ^ mask) for i in range(lax.axis_size("tile"))])


def chip_sum(grads):
    core = lax.rem(lax.axis_index("tile"), 2)
    mine = lax.dynamic_index_in_dim(grads, core, 0, False)
    other = lax.dynamic_index_in_dim(grads, 1 - core, 0, False)
    return mine + partner(other, 1)


def exchange_rows(block):
    lev = lax.axis_size("lev")
    groups = [
        [(y * 8 + rest) * lev + k for y in range(4) for k in range(lev)] for rest in range(8)
    ]
    return lax.all_to_all(
        block, ("tile", "lev"), split_axis=0, concat_axis=0, tiled=True, axis_index_groups=groups
    )


def z_sum(part):
    one, two, three = (partner(part, 2 * k) for k in (1, 2, 3))
    return (part + one) + (two + three)


def shards(state_in, east_speed, north_speed, w_in, w_out, cotangent):
    width = state_in.shape[1]
    blocks = width // ROWS
    hidden = w_in.shape[1]
    barrier = lax.optimization_barrier
    low, high = edge_rows(state_in, east_speed, cotangent)
    low, high, state_in = barrier((low, high, state_in))
    core = lax.rem(lax.axis_index("tile"), 2)
    low, high = halo(core, low, high)
    w_in_t, w_out_t = w_in.T, w_out.T
    none = jnp.zeros((3, 16, 128), F32)
    half = blocks // 2
    fields_in = (state_in, east_speed, north_speed, cotangent)
    first, back, speeds, cols_a = first_step(3 * blocks // 4, half, *fields_in, low, high, ())
    got_a = exchange(cols_a.reshape(8, width // 16, 2, 16, 128))
    held = (first, back, speeds)
    first, back, speeds, cols_b = first_step(
        blocks // 4, half, *fields_in, none, none, held
    )
    got_b = exchange(cols_b.reshape(8, width // 16, 2, 16, 128))
    outer, grads_a = network(got_a, w_in_t, w_out_t, w_in, w_out)
    outer = exchange(outer)
    inner, grads_b = network(got_b, w_in_t, w_out_t, w_in, w_out)
    part, outer = barrier((chip_sum(grads_a + grads_b), outer))
    outer = outer.reshape(width // 2, 2, 16, 128)
    quarter = width // 4

    def edge(row):
        fields = outer[(row + quarter) % width]
        return jnp.stack([first[row], back[row]]) + fields.astype(F32)

    def west(row):
        return jnp.concatenate([edge(row), speeds[row, 0][None].astype(F32)])

    part = jnp.sum(exchange_rows(part.reshape(32, hidden // 32, 128)), 0)
    part, inner, tail, head = barrier((part, inner, edge(width - 1), edge(0)))
    inner = exchange(inner).reshape(width // 2, 2, 16, 128)
    part = z_sum(jnp.stack([part, partner(part, 1)])).astype(BF16)
    low_next, high_next = halo(core, tail, head)
    low_next = jnp.concatenate([low_next, low[2:]])
    part, inner, low_next, high_next = barrier((part, inner, low_next, high_next))
    part = exchange_rows(jnp.broadcast_to(part[None], (32,) + part.shape))
    state_out, state_grad = last_step(
        0, width // LAST_ROWS, first, back, speeds, inner, outer, low_next, low_next, high_next,
        state_in.shape, (),
    )
    part, state_out, state_grad = barrier((part, state_out, state_grad))
    core = lax.rem(lax.axis_index("tile"), 2)
    in_total, out_total = totals(core.reshape(1), part)
    return state_out, state_grad, in_total, out_total


def solution(mesh):
    field = P("lev", "tile", None)
    return jax.shard_map(
        shards,
        mesh=mesh,
        in_specs=(field, field, field, P(), P(), field),
        out_specs=(field, field, P(), P()),
        check_vma=False,
    )
```

```python
import functools
import math

import jax
import jax.numpy as jnp
from jax import lax
from jax.experimental import pallas as pl
from jax.experimental.pallas import tpu as pltpu
from jax.sharding import PartitionSpec as P

KAPPA = 0.05
SLOPE_C = 0.7978845608028654
CUBIC = 0.044715
ROWS = 64
LAST_ROWS = 64
SUB = 256
UNROLL = 16
SAMPLES = 8192 * 128
F32 = jnp.float32
BF16 = jnp.bfloat16
MIB = 1024 * 1024


def spread(pairs, tile):
    for ref, scratch in pairs:
        size = min(16, ref.shape[1])
        place = pl.multiple_of(tile * 16, size)
        part = ref[:, pl.ds(place, size), :].astype(F32)
        part = jnp.swapaxes(part, 0, 1).reshape(size * 16, 128)
        scratch[pl.ds(pl.multiple_of(tile * 256, 256), size * 16), :] = part


def row(ref, index):
    return ref[pl.ds(pl.multiple_of(index * 16, 16), 16), :]


def gather(scratch, ref, rows):
    def one(tile, carry):
        part = scratch[pl.ds(pl.multiple_of(tile * 256, 256), 256), :].reshape(16, 16, 128)
        ref[:, pl.ds(pl.multiple_of(tile * 16, 16), 16), :] = jnp.swapaxes(part, 0, 1)
        return carry

    lax.fori_loop(0, rows // 16, one, 0)


def up_of(value):
    return pltpu.roll(value, value.shape[1] - 1, 1)


def down_of(value):
    return pltpu.roll(value, 1, 1)


def wall_mask(north):
    lane = lax.broadcasted_iota(jnp.int32, north.shape, 1)
    return jnp.where(lane < north.shape[1] - 1, north, 0.0)


def step_row(q, q_next, g, g_next, east, north, flux, drift):
    north = wall_mask(north)
    pos_east = jnp.maximum(east, 0.0) + KAPPA
    neg_east = jnp.minimum(east, 0.0) - KAPPA
    pos_north = jnp.maximum(north, 0.0)
    neg_north = jnp.minimum(north, 0.0)
    new_flux = pos_east * q + neg_east * q_next
    cross = pos_north * q + neg_north * up_of(q)
    moved = q - (new_flux - flux) - (cross - down_of(cross))
    ahead = g_next - g
    new_drift = neg_east * ahead
    above = up_of(g) - g
    pulled = (
        g + (pos_east * ahead + drift) + (pos_north * above + down_of(neg_north * above))
    )
    return moved, pulled, new_flux, new_drift


def west_terms(q_prev, q, g_prev, g, east_prev):
    pos = jnp.maximum(east_prev, 0.0) + KAPPA
    neg = jnp.minimum(east_prev, 0.0) - KAPPA
    return pos * q_prev + neg * q, neg * (g - g_prev)


def first_kernel(
    start, blocks, state, state_prev, state_next, cot, cot_prev, cot_next, east, east_prev,
    north, low, high, *rest,
):
    first, back, speeds, cols, q_s, g_s, east_s, north_s = rest[-13:-5]
    prev_s, gprev_s, next_s, gnext_s, eprev_s = rest[-5:]
    here = lax.rem(pl.program_id(0) + start, blocks)
    at_low = here == 0
    at_high = here == blocks - 1
    pairs = ((state, q_s), (cot, g_s), (east, east_s), (north, north_s))

    def spread_tile(tile, carry):
        spread(pairs, tile)
        return carry

    lax.fori_loop(0, ROWS // 16, spread_tile, 0)
    spread(((state_prev, prev_s), (cot_prev, gprev_s), (east_prev, eprev_s)), 0)
    spread(((state_next, next_s), (cot_next, gnext_s)), 0)
    q_prev = jnp.where(at_low, low[0], row(prev_s, 7))
    g_prev = jnp.where(at_low, low[1], row(gprev_s, 7))
    e_prev = jnp.where(at_low, low[2], row(eprev_s, 15))
    q_s[ROWS * 16 :, :] = jnp.where(at_high, high[0], row(next_s, 0))
    g_s[ROWS * 16 :, :] = jnp.where(at_high, high[1], row(gnext_s, 0))
    q = row(q_s, 0)
    g = row(g_s, 0)
    flux, drift = west_terms(q_prev, q, g_prev, g, e_prev)

    def one(i, carry):
        q, g, flux, drift = carry
        q_next = row(q_s, i + 1)
        g_next = row(g_s, i + 1)
        e = row(east_s, i)
        n = row(north_s, i)
        moved, pulled, flux, drift = step_row(q, q_next, g, g_next, e, n, flux, drift)
        first[i] = moved
        back[i] = pulled
        cols[i, 0] = moved.astype(BF16)
        cols[i, 1] = pulled.astype(BF16)
        speeds[i, 0] = e.astype(BF16)
        speeds[i, 1] = n.astype(BF16)
        return q_next, g_next, flux, drift

    lax.fori_loop(0, ROWS, one, (q, g, flux, drift), unroll=UNROLL)


def in_hbm(array):
    return pltpu.with_memory_space_constraint(array, pltpu.HBM)


def first_step(start, count, state, east, north, cot, low, high, filled):
    width = state.shape[1]
    blocks = width // ROWS
    here = lambda s: lax.rem(s + start, blocks)
    before = lambda s, size: lax.rem(here(s) * (ROWS // size) - 1 + width // size, width // size)
    after = lambda s, size: lax.rem((here(s) + 1) * (ROWS // size), width // size)
    main = pl.BlockSpec((16, ROWS, 128), lambda s: (0, here(s), 0))
    prev = pl.BlockSpec((16, 8, 128), lambda s: (0, before(s, 8), 0))
    prev16 = pl.BlockSpec((16, 16, 128), lambda s: (0, before(s, 16), 0))
    post = pl.BlockSpec((16, 8, 128), lambda s: (0, after(s, 8), 0))
    whole = lambda n: pl.BlockSpec((n, 16, 128), lambda s: (0, 0, 0))
    rows = count * ROWS
    field = pl.BlockSpec((ROWS, 16, 128), lambda s: (here(s), 0, 0))
    speed = pl.BlockSpec((ROWS, 2, 16, 128), lambda s: (here(s), 0, 0, 0))
    pair = pl.BlockSpec((ROWS, 2, 16, 128), lambda s: (s, 0, 0, 0))
    return pl.pallas_call(
        functools.partial(first_kernel, start, blocks),
        grid=(count,),
        in_specs=[main, prev, post, main, prev, post, main, prev16, main, whole(3), whole(3)]
        + [pl.BlockSpec(memory_space=pl.ANY)] * len(filled),
        out_specs=[field, field, speed, pair],
        out_shape=[
            pltpu.HBM((width, 16, 128), F32),
            pltpu.HBM((width, 16, 128), F32),
            pltpu.HBM((width, 2, 16, 128), BF16),
            pltpu.HBM((rows, 2, 16, 128), BF16),
        ],
        input_output_aliases={11 + k: k for k in range(len(filled))},
        scratch_shapes=[
            pltpu.VMEM(((ROWS + 1) * 16, 128), F32),
            pltpu.VMEM(((ROWS + 1) * 16, 128), F32),
            pltpu.VMEM((ROWS * 16, 128), F32),
            pltpu.VMEM((ROWS * 16, 128), F32),
            pltpu.VMEM((128, 128), F32),
            pltpu.VMEM((128, 128), F32),
            pltpu.VMEM((128, 128), F32),
            pltpu.VMEM((128, 128), F32),
            pltpu.VMEM((256, 128), F32),
        ],
        compiler_params=pltpu.CompilerParams(vmem_limit_bytes=16 * MIB),
        cost_estimate=pl.CostEstimate(
            flops=rows * 16 * 128 * 40, bytes_accessed=rows * 16 * 128 * 28, transcendentals=0
        ),
        name="transport_one",
    )(
        *[in_hbm(x) for x in (state, state, state, cot, cot, cot, east, east, north)],
        low,
        high,
        *filled,
    )


def edge_kernel(core, state_lo, state_hi, cot_lo, cot_hi, east_hi, by_chip, by_link):
    even = core[0] == 0
    last = (state_hi[:, 7, :], cot_hi[:, 7, :], east_hi[...].astype(F32)[:, 15, :])
    first = (state_lo[:, 0, :], cot_lo[:, 0, :], cot_lo[:, 0, :])
    for k in range(3):
        by_chip[k] = jnp.where(even, last[k], first[k])
        by_link[k] = jnp.where(even, first[k], last[k])


def edge_rows(core, state, east, cot):
    width = state.shape[1]
    head = pl.BlockSpec((16, 8, 128), lambda s: (0, 0, 0))
    tail = pl.BlockSpec((16, 8, 128), lambda s: (0, width // 8 - 1, 0))
    tail16 = pl.BlockSpec((16, 16, 128), lambda s: (0, width // 16 - 1, 0))
    return pl.pallas_call(
        edge_kernel,
        grid=(1,),
        in_specs=[pl.BlockSpec(memory_space=pltpu.SMEM), head, tail, head, tail, tail16],
        out_specs=[
            pl.BlockSpec((3, 16, 128), lambda s: (0, 0, 0)),
            pl.BlockSpec((3, 16, 128), lambda s: (0, 0, 0)),
        ],
        out_shape=[
            jax.ShapeDtypeStruct((3, 16, 128), F32),
            jax.ShapeDtypeStruct((3, 16, 128), F32),
        ],
        name="edge_rows",
    )(core, *[in_hbm(x) for x in (state, state, cot, cot, east)])


CELLS = 8
HTILE = 256


def network_kernel(cols, w_in_t, w_out_t, w_in, w_out, fields, grads, act_s, dpre_s):
    hidden = w_in_t.shape[0]

    @pl.when(pl.program_id(0) == 0)
    def _():
        grads[...] = jnp.zeros_like(grads)

    col = jnp.concatenate([cols[:, i, 0].reshape(128, 128) for i in range(CELLS)], 1)
    gcol = jnp.concatenate([cols[:, i, 1].reshape(128, 128) for i in range(CELLS)], 1)
    for h in range(0, hidden, HTILE):
        part = slice(h, h + HTILE)
        for n in range(0, CELLS * 128, SUB):
            at = slice(n, n + SUB)
            z = jnp.dot(w_in_t[part, :], col[:, at], preferred_element_type=F32)
            d_act = jnp.dot(w_out_t[part, :], gcol[:, at], preferred_element_type=F32)
            z2 = z * z
            t = jnp.tanh(z * (z2 * (SLOPE_C * CUBIC) + SLOPE_C))
            part_t = 0.5 * t
            half = part_t + 0.5
            act = z * half
            slope = half + act * (0.5 - part_t) * (
                z2 * (6.0 * SLOPE_C * CUBIC) + 2.0 * SLOPE_C
            )
            act_s[part, at] = act.astype(BF16)
            dpre_s[part, at] = (d_act * slope).astype(BF16)
    nt = (((1,), (1,)), ((), ()))
    grads[0] += lax.dot_general(dpre_s[...], col, nt, preferred_element_type=F32)
    grads[1] += lax.dot_general(act_s[...], gcol, nt, preferred_element_type=F32)
    tend = jnp.dot(w_out[...], act_s[...], preferred_element_type=F32).astype(BF16)
    d_cols = jnp.dot(w_in[...], dpre_s[...], preferred_element_type=F32).astype(BF16)
    for i in range(CELLS):
        fields[:, i, 0] = tend[:, i * 128 : (i + 1) * 128].reshape(8, 16, 128)
        fields[:, i, 1] = d_cols[:, i * 128 : (i + 1) * 128].reshape(8, 16, 128)


def network(cols, w_in_t, w_out_t, w_in, w_out):
    rows = cols.shape[1]
    hidden = w_in.shape[1]
    block = pl.BlockSpec((8, CELLS, 2, 16, 128), lambda s: (0, s, 0, 0, 0))
    tall = pl.BlockSpec((hidden, 128), lambda s: (0, 0))
    wide = pl.BlockSpec((128, hidden), lambda s: (0, 0))
    total = pl.BlockSpec((2, hidden, 128), lambda s: (0, 0, 0))
    return pl.pallas_call(
        functools.partial(network_kernel),
        grid=(rows // CELLS,),
        in_specs=[block, tall, tall, wide, wide],
        out_specs=[block, total],
        out_shape=[
            pltpu.HBM(cols.shape, BF16),
            jax.ShapeDtypeStruct((2, hidden, 128), F32),
        ],
        scratch_shapes=[
            pltpu.VMEM((hidden, CELLS * 128), BF16),
            pltpu.VMEM((hidden, CELLS * 128), BF16),
        ],
        compiler_params=pltpu.CompilerParams(vmem_limit_bytes=24 * MIB),
        cost_estimate=pl.CostEstimate(
            flops=rows * 128 * 128 * hidden * 12,
            bytes_accessed=rows * 128 * 128 * 8,
            transcendentals=rows * 128 * hidden,
        ),
        name="column_network",
    )(cols, *[in_hbm(x) for x in (w_in_t, w_out_t, w_in, w_out)])


def totals_kernel(core, sums, in_total, out_total):
    scale = 1.0 / math.sqrt(SAMPLES)
    first = core[0] == 0
    size = sums.shape[2]
    for k in range(0, sums.shape[0], 128 // size):
        pick = range(k, k + 128 // size)
        at = slice(k * size, k * size + 128)
        here = jnp.concatenate([sums[i, 0] for i in pick], 0).astype(F32).T
        there = jnp.concatenate([sums[i, 1] for i in pick], 0).astype(F32).T
        in_total[:, at] = jnp.where(first, here, there) * scale
        out_total[:, at] = jnp.where(first, there, here) * scale


def totals(core, sums):
    count, _, size, rows = sums.shape
    out = pl.BlockSpec((rows, count * size), lambda s: (0, 0))
    return pl.pallas_call(
        totals_kernel,
        grid=(1,),
        in_specs=[
            pl.BlockSpec(memory_space=pltpu.SMEM),
            pl.BlockSpec(sums.shape, lambda s: (0, 0, 0, 0)),
        ],
        out_specs=[out] * 2,
        out_shape=[pltpu.HBM((rows, count * size), F32)] * 2,
        compiler_params=pltpu.CompilerParams(vmem_limit_bytes=8 * MIB),
        name="weight_totals",
    )(core, sums)


def last_kernel(
    start, blocks, first, first_next, back, back_next, speeds, inner, inner_next, outer,
    outer_next, west, low, high, *rest,
):
    out, grad, q_s, g_s, out_s, grad_s, flux_s, drift_s = rest[-8:]
    here = lax.rem(pl.program_id(0) + start, blocks)
    quarter = blocks // 4

    def within(block):
        return jnp.logical_and(block >= quarter, block < blocks - quarter)

    def fill(fields):
        for i in range(LAST_ROWS):
            at = pl.ds(i * 16, 16)
            q_s[at, :] = first[i] + fields[i, 0].astype(F32)
            g_s[at, :] = back[i] + fields[i, 1].astype(F32)

    pl.when(within(here))(lambda: fill(inner))
    pl.when(jnp.logical_not(within(here)))(lambda: fill(outer))
    last = here == blocks - 1
    add = jnp.where(within(here + 1), inner_next[0].astype(F32), outer_next[0].astype(F32))
    q_s[LAST_ROWS * 16 :, :] = jnp.where(last, high[0], first_next[0] + add[0])
    g_s[LAST_ROWS * 16 :, :] = jnp.where(last, high[1], back_next[0] + add[1])
    q = row(q_s, 0)
    g = row(g_s, 0)
    edge = jnp.where(here == 0, low[...], west[...])
    flux, drift = west_terms(edge[0], q, edge[1], g, edge[2])
    fresh = jnp.logical_or(here == 0, pl.program_id(0) == 0)
    flux = jnp.where(fresh, flux, flux_s[...])
    drift = jnp.where(fresh, drift, drift_s[...])
    def one(i, carry):
        q, g, flux, drift = carry
        q_next = row(q_s, i + 1)
        g_next = row(g_s, i + 1)
        e = speeds[i, 0].astype(F32)
        n = speeds[i, 1].astype(F32)
        moved, pulled, flux, drift = step_row(q, q_next, g, g_next, e, n, flux, drift)
        at = pl.ds(pl.multiple_of(i * 16, 16), 16)
        out_s[at, :] = moved
        grad_s[at, :] = pulled
        return q_next, g_next, flux, drift

    carry = lax.fori_loop(0, LAST_ROWS, one, (q, g, flux, drift), unroll=UNROLL)
    flux_s[...] = carry[2]
    drift_s[...] = carry[3]
    gather(out_s, out, LAST_ROWS)
    gather(grad_s, grad, LAST_ROWS)


def last_step(start, count, first, back, speeds, inner, outer, west, low, high, shape, filled):
    width = shape[1]
    blocks = width // LAST_ROWS
    part = blocks // 4
    quarter = width // 4
    here = lambda s: lax.rem(s + start, blocks)

    def held(s):
        return jnp.clip(here(s) - part, 0, 2 * part - 1), 0, 0, 0

    def kept(s):
        b = here(s)
        return jnp.where(b < 3 * part, jnp.minimum(b + part, 2 * part - 1), b - 3 * part), 0, 0, 0

    after = lambda s: jnp.minimum((here(s) + 1) * LAST_ROWS, width - 1)

    def held_next(s):
        return jnp.clip(after(s) - quarter, 0, 2 * quarter - 1), 0, 0, 0

    def kept_next(s):
        r = after(s)
        far = jnp.clip(r - 3 * quarter, 0, 2 * quarter - 1)
        return jnp.where(r < quarter, r + quarter, far), 0, 0, 0

    field = pl.BlockSpec((LAST_ROWS, 16, 128), lambda s: (here(s), 0, 0))
    field_next = pl.BlockSpec((1, 16, 128), lambda s: (after(s), 0, 0))
    pair = lambda index: pl.BlockSpec((LAST_ROWS, 2, 16, 128), index)
    pair_next = lambda index: pl.BlockSpec((1, 2, 16, 128), index)
    whole = lambda n: pl.BlockSpec((n, 16, 128), lambda s: (0, 0, 0))
    result = pl.BlockSpec((16, LAST_ROWS, 128), lambda s: (0, here(s), 0))
    cells = count * LAST_ROWS * shape[0] * shape[2]
    return pl.pallas_call(
        functools.partial(last_kernel, start, blocks),
        grid=(count,),
        in_specs=[
            field, field_next, field, field_next, pair(lambda s: (here(s), 0, 0, 0)),
            pair(held), pair_next(held_next), pair(kept), pair_next(kept_next),
            whole(3), whole(3), whole(2),
        ]
        + [pl.BlockSpec(memory_space=pl.ANY)] * len(filled),
        out_specs=[result] * 2,
        out_shape=[pltpu.HBM(shape, F32)] * 2,
        input_output_aliases={12 + k: k for k in range(len(filled))},
        scratch_shapes=[pltpu.VMEM(((LAST_ROWS + 1) * 16, 128), F32)] * 2
        + [pltpu.VMEM((LAST_ROWS * 16, 128), F32)] * 2
        + [pltpu.VMEM((16, 128), F32)] * 2,
        compiler_params=pltpu.CompilerParams(vmem_limit_bytes=16 * MIB),
        cost_estimate=pl.CostEstimate(
            flops=cells * 40, bytes_accessed=cells * 24, transcendentals=0
        ),
        name="transport_two",
    )(
        *[in_hbm(x) for x in (first, first, back, back, speeds)],
        inner, inner, outer, outer, west, low, high, *filled,
    )


def across(block):
    count = lax.axis_size("tile")
    return lax.ppermute(
        block, "tile", [(i, (i + 1 if i % 2 else i - 1) % count) for i in range(count)]
    )


def halo(core, to_chip, to_link):
    even = core == 0
    by_link = across(to_link)
    by_chip = partner(to_chip, 1)
    return jnp.where(even, by_link, by_chip), jnp.where(even, by_chip, by_link)


def exchange(block):
    return lax.all_to_all(block, "lev", split_axis=0, concat_axis=0, tiled=True)


def partner(block, mask):
    return lax.ppermute(block, "tile", [(i, i ^ mask) for i in range(lax.axis_size("tile"))])


def chip_sum(grads):
    core = lax.rem(lax.axis_index("tile"), 2)
    mine = lax.dynamic_index_in_dim(grads, core, 0, False)
    other = lax.dynamic_index_in_dim(grads, 1 - core, 0, False)
    return mine + partner(other, 1)


def exchange_rows(block):
    lev = lax.axis_size("lev")
    groups = [
        [(y * 8 + rest) * lev + k for y in range(4) for k in range(lev)] for rest in range(8)
    ]
    return lax.all_to_all(
        block, ("tile", "lev"), split_axis=0, concat_axis=0, tiled=True, axis_index_groups=groups
    )


def z_sum(part):
    one, two, three = (partner(part, 2 * k) for k in (1, 2, 3))
    return (part + one) + (two + three)


def shards(state_in, east_speed, north_speed, w_in, w_out, cotangent):
    width = state_in.shape[1]
    blocks = width // ROWS
    hidden = w_in.shape[1]
    barrier = lax.optimization_barrier
    core = lax.rem(lax.axis_index("tile"), 2)
    to_chip, to_link = edge_rows(core.reshape(1), state_in, east_speed, cotangent)
    to_chip, to_link, state_in = barrier((to_chip, to_link, state_in))
    low, high = halo(core, to_chip, to_link)
    w_in_t, w_out_t = w_in.T, w_out.T
    none = jnp.zeros((3, 16, 128), F32)
    half = blocks // 2
    fields_in = (state_in, east_speed, north_speed, cotangent)
    first, back, speeds, cols_a = first_step(3 * blocks // 4, half, *fields_in, low, high, ())
    got_a = exchange(cols_a.reshape(8, width // 16, 2, 16, 128))
    held = (first, back, speeds)
    first, back, speeds, cols_b = first_step(
        blocks // 4, half, *fields_in, none, none, held
    )
    got_b = exchange(cols_b.reshape(8, width // 16, 2, 16, 128))
    outer, grads_a = network(got_a, w_in_t, w_out_t, w_in, w_out)
    outer = exchange(outer)
    inner, grads_b = network(got_b, w_in_t, w_out_t, w_in, w_out)
    part, outer = barrier((chip_sum(grads_a + grads_b), outer))
    outer = outer.reshape(width // 2, 2, 16, 128)
    quarter = width // 4

    def edge(row):
        fields = outer[(row + quarter) % width]
        return jnp.stack([first[row], back[row]]) + fields.astype(F32)

    def west(row):
        return jnp.concatenate([edge(row), speeds[row, 0][None].astype(F32)])

    part = jnp.sum(exchange_rows(part.reshape(32, hidden // 32, 128)), 0)
    part, inner, tail, head = barrier((part, inner, edge(width - 1), edge(0)))
    inner = exchange(inner).reshape(width // 2, 2, 16, 128)
    part = z_sum(jnp.stack([part, partner(part, 1)])).astype(BF16)
    low_next, high_next = halo(
        core, jnp.where(core == 0, tail, head), jnp.where(core == 0, head, tail)
    )
    low_next = jnp.concatenate([low_next, low[2:]])
    part, inner, low_next, high_next = barrier((part, inner, low_next, high_next))
    part = exchange_rows(jnp.broadcast_to(part[None], (32,) + part.shape))
    state_out, state_grad = last_step(
        0, width // LAST_ROWS, first, back, speeds, inner, outer, low_next, low_next, high_next,
        state_in.shape, (),
    )
    part, state_out, state_grad = barrier((part, state_out, state_grad))
    core = lax.rem(lax.axis_index("tile"), 2)
    in_total, out_total = totals(core.reshape(1), part)
    return state_out, state_grad, in_total, out_total


def solution(mesh):
    field = P("lev", "tile", None)
    return jax.shard_map(
        shards,
        mesh=mesh,
        in_specs=(field, field, field, P(), P(), field),
        out_specs=(field, field, P(), P()),
        check_vma=False,
    )
```
